512 devices in a mesh: section: 16 (over z, core), chan: 32 (over x, y).
Axes of the slice: x: 4, y: 8, z: 8, core: 2. Of those that a mesh axis runs over, the one named last changes fastest.
Arguments:
- opening_level_feeds: bfloat16 [16, 256, 2048], P('section', None, 'chan'), may hold values from -6 to 6
- newcomer_embeddings: bfloat16 [3, 256, 2048], P(None, None, 'chan'), may hold values from -6 to 6
- occupied_positions_per_piece: int32 [19], replicated, may hold values from 1 to 256, 3648 in all
- rootmean_gain_matrix: float32 [16, 2048], P('section'), may hold values from 0.5 to 1.5
- payload_projection_matrix: bfloat16 [16, 2048, 2048], P('section', None, 'chan'), may hold values from -0.125 to 0.125
- interior_multiplier_matrix: bfloat16 [16, 2048, 2048], P('section', None, 'chan'), may hold values from -0.125 to 0.125
- exterior_multiplier_matrix: bfloat16 [16, 2048, 2048], P('section', None, 'chan'), may hold values from -0.125 to 0.125
- emission_projection_matrix: bfloat16 [16, 2048, 2048], P('section', None, 'chan'), may hold values from -0.125 to 0.125
- bypass_channel_factors: float32 [16, 2048], P('section', 'chan'), may hold values from 0.5 to 1.5
- kernel_spectra_by_delay: float32 [16, 4, 2, 2048, 512], P('section', None, None, 'chan'), may hold values from -3 to 3
- archived_block_spectra: float32 [16, 3, 2, 2048, 512], P('section', None, None, 'chan'), may hold values from -96 to 96
Outputs:
- layer_out: bfloat16 [16, 4, 256, 2048], P('section', None, None, 'chan')
The draws below stay inside these ranges and needn't reach their ends.
Inputs may be any that keep to these rules, and one draw needn't show every extreme that they name: `occupied_positions_per_piece`: every slice has at least one live token; the longest has exactly 256.
All inputs are finite; a program needn't handle non-finite values.
Results may differ from the reference program's by a relative error of at most 0.015.
Values may be sent and summed in bfloat16 or wider, within the bound.
No kernel may reach another device: no remote copies, remote signals or barrier semaphores. Data moves between devices by JAX's collectives and lax.ppermute only.
A program may use at most 64 MiB of HBM per device.

```python
import math
import jax
import jax.numpy as jnp
import numpy as np
from jax import lax

CHANNEL_BREADTH = 2048
POSITION_CAPACITY = 256
NB = 3
TICKS = 4
PERIOD = 512
DEPTH_TOTAL = 16
SLICES = 19


def levels(key, dims, shards, smallest, high):
    factor_of = 1.0
    for axis_at, parts in shards:
        steps = jax.random.uniform(jax.random.fold_in(jax.random.fold_in(key, 6), axis_at), (parts,), jnp.float32, smallest / len(shards), high / len(shards))
        factor_of = factor_of * jnp.repeat(jnp.exp(steps), dims[axis_at] // parts).reshape((-1,) + (1,) * (len(dims) - 1 - axis_at))
    return factor_of


def split_up(count, total, bound, slope):
    loads = [(1 << 20) // math.isqrt(standing ** slope) + 1 for standing in range(2, count + 1)]
    rest, counts = total - bound - (count - 1), [1] * (count - 1)
    while rest > 0:
        free = [i for i in range(count - 1) if counts[i] < bound]
        mass, budget = sum([loads[i] for i in free]), rest
        for i in free:
            more = min(bound - counts[i], max(1, budget * loads[i] // mass), rest)
            counts[i] = counts[i] + more
            rest = rest - more
    return np.array([bound] + counts)


def uneven_parts(stream_key, number_of, total, reach, lean):
    if number_of == 2:
        one = jax.random.randint(stream_key, (), max(1, total - reach), min(reach, total - 1) + 1)
        return jnp.stack([one, total - one])
    lengths = jnp.asarray(split_up(number_of, total, reach, lean), jnp.int32)
    couples = (number_of - 1) // 2
    source_of, sink = lengths[1:1 + 2 * couples:2], lengths[2:2 + 2 * couples:2]
    margin = jnp.minimum(source_of - 1, reach - sink)
    passed = jax.random.randint(jax.random.fold_in(stream_key, 1), (couples,), 0, 1 << 20) % (margin + 1)
    lengths = lengths.at[1:1 + 2 * couples:2].set(source_of - passed).at[2:2 + 2 * couples:2].set(sink + passed)
    return lengths[jax.random.permutation(jax.random.fold_in(stream_key, 2), number_of)]


def centred(key, dims, width, reach, pieces=(), held_as=jnp.bfloat16):
    drawn = width * jax.random.normal(key, dims, jnp.float32)
    if pieces:
        drawn = drawn * levels(key, dims, pieces, -0.22, 0.18)
    return jnp.clip(drawn, -reach, reach).astype(held_as)


def setup_inputs(seed: int = 0) -> dict:
    key_list = jax.random.split(jax.random.key(seed), 12)
    opening_level_feeds = centred(key_list[0], (DEPTH_TOTAL, POSITION_CAPACITY, CHANNEL_BREADTH), 1.0, 6.0, ((0, 16), (2, 32)))
    newcomer_embeddings = centred(key_list[1], (TICKS - 1, POSITION_CAPACITY, CHANNEL_BREADTH), 1.0, 6.0, ((2, 32),))
    occupied_positions_per_piece = uneven_parts(key_list[2], SLICES, SLICES * POSITION_CAPACITY * 3 // 4, POSITION_CAPACITY, 1).astype(jnp.int32)
    rootmean_gain_matrix = jnp.clip(1.0 + 0.1 * jax.random.normal(key_list[3], (DEPTH_TOTAL, CHANNEL_BREADTH), jnp.float32), 0.5, 1.5)
    payload_projection_matrix = centred(key_list[4], (DEPTH_TOTAL, CHANNEL_BREADTH, CHANNEL_BREADTH), CHANNEL_BREADTH ** -0.5, 0.125, ((0, 16), (2, 32)))
    interior_multiplier_matrix = centred(key_list[5], (DEPTH_TOTAL, CHANNEL_BREADTH, CHANNEL_BREADTH), CHANNEL_BREADTH ** -0.5, 0.125, ((0, 16), (2, 32)))
    exterior_multiplier_matrix = centred(key_list[6], (DEPTH_TOTAL, CHANNEL_BREADTH, CHANNEL_BREADTH), CHANNEL_BREADTH ** -0.5, 0.125, ((0, 16), (2, 32)))
    emission_projection_matrix = centred(key_list[7], (DEPTH_TOTAL, CHANNEL_BREADTH, CHANNEL_BREADTH), CHANNEL_BREADTH ** -0.5, 0.125, ((0, 16), (2, 32)))
    bypass_channel_factors = jnp.clip(0.5 + 1.0 * jax.random.uniform(key_list[8], (DEPTH_TOTAL, CHANNEL_BREADTH), jnp.float32) ** levels(key_list[8], (DEPTH_TOTAL, CHANNEL_BREADTH), ((0, 16), (1, 32)), -0.2, 0.2), 0.5, 1.5)
    kernel_spectra_by_delay = centred(key_list[9], (DEPTH_TOTAL, NB + 1, 2, CHANNEL_BREADTH, PERIOD), 0.5, 3.0, ((0, 16), (3, 32)), jnp.float32)
    archived_block_spectra = centred(key_list[10], (DEPTH_TOTAL, NB, 2, CHANNEL_BREADTH, PERIOD), (POSITION_CAPACITY ** 0.5), 96.0, ((0, 16), (3, 32)), jnp.float32)
    return dict(opening_level_feeds=opening_level_feeds, newcomer_embeddings=newcomer_embeddings, occupied_positions_per_piece=occupied_positions_per_piece, rootmean_gain_matrix=rootmean_gain_matrix, payload_projection_matrix=payload_projection_matrix, interior_multiplier_matrix=interior_multiplier_matrix, exterior_multiplier_matrix=exterior_multiplier_matrix, emission_projection_matrix=emission_projection_matrix, bypass_channel_factors=bypass_channel_factors, kernel_spectra_by_delay=kernel_spectra_by_delay, archived_block_spectra=archived_block_spectra)


highest = lax.Precision.HIGHEST

def tables(length, period):
    rows_index = jnp.arange(length, dtype=jnp.int32)[:, None]
    freq_index = jnp.arange(period, dtype=jnp.int32)[None, :]
    phase = rows_index * freq_index % period
    angle = phase.astype(jnp.float32) * (2.0 * math.pi / period)
    return (jnp.cos(angle), jnp.sin(angle))

def forward_spectrum(driven, cos_table, sin_table):
    contract = (((0,), (0,)), ((), ()))
    real_part = lax.dot_general(driven, cos_table, contract, precision=highest, preferred_element_type=jnp.float32)
    imag_part = -lax.dot_general(driven, sin_table, contract, precision=highest, preferred_element_type=jnp.float32)
    return (real_part, imag_part)

def inverse_rows(zreal, zimag, cos_table, sin_table):
    contract = (((1,), (1,)), ((), ()))
    cosine_part = lax.dot_general(cos_table, zreal, contract, precision=highest, preferred_element_type=jnp.float32)
    sine_part = lax.dot_general(sin_table, zimag, contract, precision=highest, preferred_element_type=jnp.float32)
    return (cosine_part - sine_part) / cos_table.shape[1]

def spectral_mix(spectrum, lagged, filter_spec):
    zreal = filter_spec[0, 0] * spectrum[0] - filter_spec[0, 1] * spectrum[1]
    zimag = filter_spec[0, 0] * spectrum[1] + filter_spec[0, 1] * spectrum[0]
    for lag_index in range(len(lagged)):
        earlier = lagged[lag_index]
        zreal = zreal + (filter_spec[lag_index + 1, 0] * earlier[0] - filter_spec[lag_index + 1, 1] * earlier[1])
        zimag = zimag + (filter_spec[lag_index + 1, 0] * earlier[1] + filter_spec[lag_index + 1, 1] * earlier[0])
    return (zreal, zimag)

def reference(opening_level_feeds, newcomer_embeddings, occupied_positions_per_piece, rootmean_gain_matrix, payload_projection_matrix, interior_multiplier_matrix, exterior_multiplier_matrix, emission_projection_matrix, bypass_channel_factors, kernel_spectra_by_delay, archived_block_spectra):
    cos_table, sin_table = tables(POSITION_CAPACITY, PERIOD)
    positions = jnp.arange(POSITION_CAPACITY, dtype=jnp.int32)[:, None]
    results = [[] for active_level_number in range(DEPTH_TOTAL)]
    spectra = [[] for active_level_number in range(DEPTH_TOTAL)]
    for tick in range(TICKS):
        for active_level_number in range(DEPTH_TOTAL):
            if tick == 0:
                level_feed = opening_level_feeds[active_level_number]
            elif active_level_number == 0:
                level_feed = newcomer_embeddings[tick - 1]
            else:
                level_feed = results[active_level_number - 1][tick - 1]
            slice_index = tick - active_level_number + DEPTH_TOTAL - 1
            live = positions < occupied_positions_per_piece[slice_index]
            u_wide = level_feed.astype(jnp.float32)
            scale = lax.rsqrt(lax.optimization_barrier(jnp.mean(u_wide * u_wide, axis=1, keepdims=True)) + 1e-06)
            normed = (u_wide * scale * rootmean_gain_matrix[active_level_number][None, :]).astype(jnp.bfloat16)
            value = jnp.dot(normed, payload_projection_matrix[active_level_number], preferred_element_type=jnp.float32)
            gate_in = jnp.dot(normed, interior_multiplier_matrix[active_level_number], preferred_element_type=jnp.float32)
            gate_out = jnp.dot(normed, exterior_multiplier_matrix[active_level_number], preferred_element_type=jnp.float32)
            driven = jnp.where(live, gate_in * value, jnp.float32(0.0))
            spectrum = forward_spectrum(driven, cos_table, sin_table)
            lagged = []
            for lag in range(1, NB + 1):
                if lag <= tick:
                    lagged.append(spectra[active_level_number][tick - lag])
                else:
                    lagged.append((archived_block_spectra[active_level_number, lag - tick - 1, 0], archived_block_spectra[active_level_number, lag - tick - 1, 1]))
            spectra[active_level_number].append(spectrum)
            zreal, zimag = spectral_mix(spectrum, lagged, kernel_spectra_by_delay[active_level_number])
            conv = inverse_rows(zreal, zimag, cos_table, sin_table)
            mixed = (gate_out * (conv + bypass_channel_factors[active_level_number][None, :] * driven)).astype(jnp.bfloat16)
            out_rows = (u_wide + jnp.dot(mixed, emission_projection_matrix[active_level_number], preferred_element_type=jnp.float32)).astype(jnp.bfloat16)
            results[active_level_number].append(out_rows)
    return jnp.stack([jnp.stack(results[active_level_number], axis=0) for active_level_number in range(DEPTH_TOTAL)], axis=0)
```

```python
import functools

import jax
import jax.numpy as jnp
import numpy as np
from jax import lax
from jax.experimental import pallas as pl
from jax.experimental.pallas import tpu as pltpu
from jax.sharding import Mesh
from jax.sharding import PartitionSpec as P

SECTION = ("z", "core")


def params(cost=None):
    return pltpu.CompilerParams(vmem_limit_bytes=48 * 1024 * 1024)


def tables(length, period):
    phase = np.arange(length)[:, None] * np.arange(period)[None, :] % period
    angle = phase * (2.0 * np.pi / period)
    forward = np.concatenate([np.cos(angle), -np.sin(angle)], axis=1)
    return forward.astype(jnp.bfloat16), (forward.T / period).astype(jnp.bfloat16)


def spread(block, axis):
    n = lax.axis_size(axis)
    copies = jnp.broadcast_to(block[None], (n,) + block.shape)
    got = lax.all_to_all(copies, axis, 0, 0, tiled=True)
    return got.reshape((n * block.shape[0],) + block.shape[1:])


def mix_kernel(tick, blocks, length_ref, u_ref, w_ref, fwd_ref, inv_ref, filt_ref, skip_ref, *rest):
    held = rest[: blocks - min(tick, blocks)]
    past = rest[len(held) : len(held) + min(tick, blocks)]
    mixed_ref, spec_ref = rest[len(held) + len(past) :]
    width, positions = mixed_ref.shape
    period = fwd_ref.shape[1] // 2
    u = u_ref[...]
    wide = u.astype(jnp.float32)
    square = jnp.sum(wide * wide, axis=0, keepdims=True) * (1.0 / u.shape[0])
    scale = lax.rsqrt(square + 1e-06)
    gates = jnp.dot(w_ref[...], u, preferred_element_type=jnp.float32) * scale
    live = lax.broadcasted_iota(jnp.int32, (1, positions), 1) < length_ref[0]
    driven = jnp.where(live, gates[width : 2 * width] * gates[:width], 0.0)
    spectrum = jnp.dot(driven.astype(jnp.bfloat16), fwd_ref[...], preferred_element_type=jnp.float32)
    real, imag = spectrum[:, :period], spectrum[:, period:]
    spec_ref[0] = real
    spec_ref[1] = imag
    zreal = filt_ref[0, 0] * real - filt_ref[0, 1] * imag
    zimag = filt_ref[0, 0] * imag + filt_ref[0, 1] * real
    for lag, ref in enumerate(past + held, 1):
        zreal += filt_ref[lag, 0] * ref[0] - filt_ref[lag, 1] * ref[1]
        zimag += filt_ref[lag, 0] * ref[1] + filt_ref[lag, 1] * ref[0]
    packed = jnp.concatenate([zreal, zimag], axis=1).astype(jnp.bfloat16)
    conv = jnp.dot(packed, inv_ref[...], preferred_element_type=jnp.float32)
    mixed_ref[...] = (gates[2 * width :] * (conv + skip_ref[...] * driven)).astype(mixed_ref.dtype)


def mix(tick, blocks, length, u, weights, forward, inverse, filters, skip, held, past):
    width, positions = skip.shape[0], u.shape[1]
    vmem = pl.BlockSpec(memory_space=pltpu.VMEM)
    operands = [u, weights, forward, inverse, filters, skip] + held + past
    return pl.pallas_call(
        functools.partial(mix_kernel, tick, blocks),
        out_shape=(
            jax.ShapeDtypeStruct((width, positions), jnp.bfloat16),
            jax.ShapeDtypeStruct((2, width, filters.shape[-1]), jnp.float32),
        ),
        in_specs=[pl.BlockSpec(memory_space=pltpu.SMEM)] + [vmem] * len(operands),
        out_specs=(vmem, vmem),
        compiler_params=params(),
        name="mix",
    )(length, *operands)


def emit_kernel(w_ref, mixed_ref, u_ref, out_ref):
    total = jnp.dot(w_ref[...], mixed_ref[...], preferred_element_type=jnp.float32)
    out_ref[...] = (u_ref[...].astype(jnp.float32) + total).astype(out_ref.dtype)


def emit(weights, mixed, u):
    vmem = pl.BlockSpec(memory_space=pltpu.VMEM)
    return pl.pallas_call(
        emit_kernel,
        out_shape=jax.ShapeDtypeStruct(u.shape, jnp.bfloat16),
        in_specs=[vmem] * 3,
        out_specs=vmem,
        compiler_params=params(),
        name="emit",
    )(weights, mixed, u)


def local(feeds, newcomers, occupied, gain, value_w, in_w, out_w, emit_w, skip, filters, archive):
    section = lax.axis_index(SECTION)
    layers = lax.axis_size(SECTION)
    ticks = newcomers.shape[0] + 1
    blocks = archive.shape[1]
    positions, width = feeds.shape[1:]
    row = lax.axis_index("y")
    forward, inverse = (jnp.asarray(t) for t in tables(positions, filters.shape[-1]))

    emit_t = emit_w[0].T
    depth = emit_t.shape[1]
    fresh = newcomers.transpose(2, 0, 1).reshape(width, -1)
    shared = lax.all_gather(jnp.concatenate([emit_t, fresh], axis=1), "y", axis=0, tiled=True)
    emit_rows = shared[:, :depth]

    weights = jnp.concatenate([value_w[0].T, in_w[0].T, out_w[0].T], axis=0).astype(jnp.float32)
    weights = (weights * gain).astype(jnp.bfloat16)
    skip_column = skip[0][:, None]

    pairs = [(i, i + 1) for i in range(layers - 1)]
    outputs, spectra = [], []
    part = spread(feeds[0].T, "y")
    for tick in range(ticks):
        u = spread(part, "x")
        length = lax.dynamic_slice_in_dim(occupied, tick - section + layers - 1, 1, 0)
        held = [archive[0, i] for i in range(blocks - min(tick, blocks))]
        mixed, spectrum = mix(
            tick, blocks, length, u, weights, forward, inverse, filters[0], skip_column, held, spectra[::-1][:blocks]
        )
        spectra.append(spectrum)
        mixed = spread(spread(mixed, "y"), "x")
        if tick < ticks - 1:
            part = emit(emit_rows, mixed, part)
            outputs.append(lax.dynamic_slice_in_dim(part, row * width, width, 0))
            arriving = lax.ppermute(part, SECTION, pairs)
            newcomer = shared[:, depth + tick * positions : depth + (tick + 1) * positions]
            part = jnp.where(section == 0, newcomer, arriving)
        else:
            own = lax.dynamic_slice_in_dim(part, row * width, width, 0)
            outputs.append(emit(emit_t, mixed, own))
    return jnp.stack(outputs, axis=0).transpose(0, 2, 1)[None]


def solution(mesh):
    grid = Mesh(mesh.devices.reshape(8, 2, 4, 8), ("z", "core", "x", "y"))
    chan = ("x", "y")
    return jax.shard_map(
        local,
        mesh=grid,
        in_specs=(
            P(SECTION, None, chan),
            P(None, None, chan),
            P(),
            P(SECTION, None),
            P(SECTION, None, chan),
            P(SECTION, None, chan),
            P(SECTION, None, chan),
            P(SECTION, None, chan),
            P(SECTION, chan),
            P(SECTION, None, None, chan, None),
            P(SECTION, None, None, chan, None),
        ),
        out_specs=P(SECTION, None, None, chan),
        check_vma=False,
    )
```

```python
import functools

import jax
import jax.numpy as jnp
import numpy as np
from jax import lax
from jax.experimental import pallas as pl
from jax.experimental.pallas import tpu as pltpu
from jax.sharding import Mesh
from jax.sharding import PartitionSpec as P

SECTION = ("z", "core")
EXTRA = 16


def call(body, out, operands, name, smem=0):
    vmem = pl.BlockSpec(memory_space=pltpu.VMEM)
    scalars = pl.BlockSpec(memory_space=pltpu.SMEM)
    return pl.pallas_call(
        body,
        out_shape=out,
        in_specs=[scalars] * smem + [vmem] * (len(operands) - smem),
        out_specs=jax.tree.map(lambda _: vmem, out),
        compiler_params=pltpu.CompilerParams(vmem_limit_bytes=40 * 1024 * 1024),
        name=name,
    )(*operands)


def tables(length, period):
    phase = np.arange(length)[:, None] * np.arange(period)[None, :] % period
    angle = phase * (2.0 * np.pi / period)
    forward = np.concatenate([np.cos(angle), -np.sin(angle)], axis=1)
    return forward.astype(jnp.bfloat16), (forward.T / period).astype(jnp.bfloat16)


def swap(blocks, axis):
    return lax.all_to_all(blocks, axis, 0, 0, tiled=True)


def gather_rows(copies):
    got = swap(copies, "y")
    return got.reshape((-1, got.shape[-1]))


def gate_terms_kernel(w_ref, gain_ref, u_ref, out_ref):
    groups, rows, positions = out_ref.shape
    rows -= EXTRA
    u = u_ref[...].astype(jnp.float32)
    square = jnp.sum(u * u, axis=0, keepdims=True)
    upper = square.astype(jnp.bfloat16).astype(jnp.float32)
    at = lax.broadcasted_iota(jnp.int32, (EXTRA, positions), 0)
    extra = jnp.where(at == 0, upper, jnp.where(at == 1, square - upper, 0.0)).astype(out_ref.dtype)
    scaled = u * gain_ref[...]
    high = scaled.astype(jnp.bfloat16)
    low = (scaled - high.astype(jnp.float32)).astype(jnp.bfloat16)
    for x in range(groups):
        w = w_ref[x, :rows]
        term = jnp.dot(w, high, preferred_element_type=jnp.float32)
        term += jnp.dot(w, low, preferred_element_type=jnp.float32)
        out_ref[x, :rows] = term.astype(out_ref.dtype)
        out_ref[x, rows:] = extra


def mix_kernel(past, features, length_ref, terms_ref, fwd_ref, inv_ref, filt_ref, skip_ref, *rest):
    lagged, (mixed_ref, spec_ref) = rest[:-2], rest[-2:]
    copies, width, positions = mixed_ref.shape
    period = fwd_ref.shape[1] // 2
    terms = jnp.sum(terms_ref[...].astype(jnp.float32), axis=0)
    square = terms[3 * width : 3 * width + 1] + terms[3 * width + 1 : 3 * width + 2]
    gates = terms[: 3 * width] * lax.rsqrt(square * (1.0 / features) + 1e-06)
    live = lax.broadcasted_iota(jnp.int32, (1, positions), 1) < length_ref[0]
    driven = jnp.where(live, gates[width : 2 * width] * gates[:width], 0.0)
    spectrum = jnp.dot(driven.astype(jnp.bfloat16), fwd_ref[...], preferred_element_type=jnp.float32)
    real, imag = spectrum[:, :period], spectrum[:, period:]
    spec_ref[0] = real
    spec_ref[1] = imag
    zreal = filt_ref[0, 0] * real - filt_ref[0, 1] * imag
    zimag = filt_ref[0, 0] * imag + filt_ref[0, 1] * real
    for lag, ref in enumerate(lagged, 1):
        if lag <= past:
            first, second = ref[0], ref[1]
        else:
            first, second = ref[lag - past - 1, 0], ref[lag - past - 1, 1]
        zreal += filt_ref[lag, 0] * first - filt_ref[lag, 1] * second
        zimag += filt_ref[lag, 0] * second + filt_ref[lag, 1] * first
    packed = jnp.concatenate([zreal, zimag], axis=1).astype(jnp.bfloat16)
    conv = jnp.dot(packed, inv_ref[...], preferred_element_type=jnp.float32)
    mixed = (gates[2 * width :] * (conv + skip_ref[...] * driven)).astype(mixed_ref.dtype)
    for y in range(copies):
        mixed_ref[y] = mixed


def emit_terms_kernel(w_ref, mixed_ref, out_ref):
    groups, rows, _ = out_ref.shape
    mixed = mixed_ref[...]
    for x in range(groups):
        w = w_ref[x, w_ref.shape[1] - rows :]
        out_ref[x] = jnp.dot(w, mixed, preferred_element_type=jnp.float32).astype(out_ref.dtype)


def add_kernel(terms_ref, own_ref, out_ref):
    total = own_ref[...].astype(jnp.float32) + jnp.sum(terms_ref[...].astype(jnp.float32), axis=0)
    out_ref[...] = total.astype(out_ref.dtype)


def add_and_send_kernel(last_ref, terms_ref, own_ref, fresh_ref, out_ref, send_ref):
    add_kernel(terms_ref, own_ref, out_ref)
    send_ref[...] = jnp.where(last_ref[0] == 1, fresh_ref[...], out_ref[...])


def local(feeds, newcomers, occupied, gain, value_w, in_w, out_w, emit_w, skip, filters, archive):
    section = lax.axis_index(SECTION)
    layers = lax.axis_size(SECTION)
    groups, copies = lax.axis_size("x"), lax.axis_size("y")
    ticks = newcomers.shape[0] + 1
    blocks = archive.shape[1]
    positions, width = feeds.shape[1:]
    features = gain.shape[1]
    rows = features // groups
    bf16 = functools.partial(jax.ShapeDtypeStruct, dtype=jnp.bfloat16)
    f32 = functools.partial(jax.ShapeDtypeStruct, dtype=jnp.float32)
    forward, inverse = (jnp.asarray(t) for t in tables(positions, filters.shape[-1]))

    own = feeds[0].T
    part = gather_rows(jnp.broadcast_to(own[None], (copies,) + own.shape))
    weights = jnp.concatenate([value_w[0], in_w[0], out_w[0], emit_w[0]], axis=1).T
    weights = swap(weights.reshape(-1, groups, rows).transpose(1, 0, 2), "x")
    gain_column = lax.dynamic_slice_in_dim(gain[0], lax.axis_index("x") * rows, rows, 0)[:, None]
    skip_column = skip[0][:, None]
    fresh = newcomers.transpose(0, 2, 1)
    last = (section == layers - 1).astype(jnp.int32)[None]

    ring = [(i, (i + 1) % layers) for i in range(layers)]
    outputs, spectra = [], []
    for tick in range(ticks):
        terms = call(
            gate_terms_kernel,
            bf16((groups, 3 * width + EXTRA, positions)),
            [weights, gain_column, part],
            "gate_terms",
        )
        terms = swap(terms, "x")
        length = lax.dynamic_slice_in_dim(occupied, tick - section + layers - 1, 1, 0)
        past = min(tick, blocks)
        lagged = spectra[::-1][:past] + [archive[0]] * (blocks - past)
        mixed, spectrum = call(
            functools.partial(mix_kernel, past, features),
            (bf16((copies, width, positions)), f32((2, width, filters.shape[-1]))),
            [length, terms, forward, inverse, filters[0], skip_column] + lagged,
            "mix",
            smem=1,
        )
        spectra.append(spectrum)
        terms = call(
            emit_terms_kernel,
            bf16((groups, width, positions)),
            [weights, gather_rows(mixed)],
            "emit_terms",
        )
        terms = swap(terms, "x")
        if tick < ticks - 1:
            out, send = call(
                add_and_send_kernel, (bf16(own.shape), bf16(own.shape)), [last, terms, own, fresh[tick]], "add", smem=1
            )
            own = lax.ppermute(send, SECTION, ring)
            part = gather_rows(jnp.broadcast_to(own[None], (copies,) + own.shape))
        else:
            out = call(add_kernel, bf16(own.shape), [terms, own], "add")
        outputs.append(out)
    return jnp.stack(outputs, axis=0).transpose(0, 2, 1)[None]


def solution(mesh):
    grid = Mesh(mesh.devices.reshape(8, 2, 4, 8), ("z", "core", "x", "y"))
    chan = ("x", "y")
    return jax.shard_map(
        local,
        mesh=grid,
        in_specs=(
            P(SECTION, None, chan),
            P(None, None, chan),
            P(),
            P(SECTION, None),
            P(SECTION, None, chan),
            P(SECTION, None, chan),
            P(SECTION, None, chan),
            P(SECTION, None, chan),
            P(SECTION, chan),
            P(SECTION, None, None, chan, None),
            P(SECTION, None, None, chan, None),
        ),
        out_specs=P(SECTION, None, None, chan),
        check_vma=False,
    )
```

```python
import functools

import jax
import jax.numpy as jnp
import numpy as np
from jax import lax
from jax.experimental import pallas as pl
from jax.experimental.pallas import tpu as pltpu
from jax.sharding import Mesh
from jax.sharding import PartitionSpec as P

SECTION = ("z", "core")
EXTRA = 16


def call(body, out, operands, name, smem=0):
    vmem = pl.BlockSpec(memory_space=pltpu.VMEM)
    scalars = pl.BlockSpec(memory_space=pltpu.SMEM)
    return pl.pallas_call(
        body,
        out_shape=out,
        in_specs=[scalars] * smem + [vmem] * (len(operands) - smem),
        out_specs=jax.tree.map(lambda _: vmem, out),
        compiler_params=pltpu.CompilerParams(vmem_limit_bytes=40 * 1024 * 1024),
        name=name,
    )(*operands)


def tables(length, period):
    phase = np.arange(length)[:, None] * np.arange(period)[None, :] % period
    angle = phase * (2.0 * np.pi / period)
    forward = np.concatenate([np.cos(angle), -np.sin(angle)], axis=1)
    return forward.astype(jnp.bfloat16), (forward.T / period).astype(jnp.bfloat16)


def swap(blocks, axis):
    return lax.all_to_all(blocks, axis, 0, 0, tiled=True)


def gather_rows(copies):
    got = swap(copies, "y")
    return got.reshape((-1, got.shape[-1]))


def deal_kernel(x_ref, gain_ref, *refs):
    matrices, blocks = refs[: len(refs) // 2], refs[len(refs) // 2 :]
    groups = len(blocks)
    width = matrices[0].shape[0]
    rows = blocks[0].shape[1]
    for step, block in enumerate(blocks):
        start = lax.rem(x_ref[0] + step, groups) * rows
        at = pl.ds(pl.multiple_of(start, rows), rows)
        gain = gain_ref[:, at]
        for m, matrix in enumerate(matrices):
            w = matrix[:, at]
            if m < len(matrices) - 1:
                w = (w.astype(jnp.float32) * gain).astype(w.dtype)
            block[m * width : (m + 1) * width] = w


def history_kernel(filt_ref, held_ref, fwd_ref, inv_ref, known_ref, filt_out, fwd_out, inv_out):
    blocks = held_ref.shape[0]
    for tick in range(blocks):
        real = imag = 0.0
        for lag in range(tick + 1, blocks + 1):
            held = held_ref.at[lag - tick - 1]
            real += filt_ref[lag, 0] * held[0] - filt_ref[lag, 1] * held[1]
            imag += filt_ref[lag, 0] * held[1] + filt_ref[lag, 1] * held[0]
        known_ref[tick, 0] = real
        known_ref[tick, 1] = imag
    filt_out[...] = filt_ref[...]
    fwd_out[...] = fwd_ref[...]
    inv_out[...] = inv_ref[...]


def gate_terms_kernel(x_ref, u_ref, *refs):
    blocks, out_ref = refs[:-1], refs[-1]
    groups, rows, positions = out_ref.shape
    rows -= EXTRA
    u = u_ref[...]
    wide = u.astype(jnp.float32)
    square = jnp.sum(wide * wide, axis=0, keepdims=True)
    upper = square.astype(jnp.bfloat16).astype(jnp.float32)
    at = lax.broadcasted_iota(jnp.int32, (EXTRA, positions), 0)
    extra = jnp.where(at == 0, upper, jnp.where(at == 1, square - upper, 0.0)).astype(out_ref.dtype)
    for step, block in enumerate(blocks):
        x = lax.rem(x_ref[0] + groups - step, groups)
        term = jnp.dot(block[:rows], u, preferred_element_type=jnp.float32)
        out_ref[x, :rows] = term.astype(out_ref.dtype)
        out_ref[x, rows:] = extra


def mix_kernel(past, stored, features, length_ref, terms_ref, fwd_ref, inv_ref, filt_ref, skip_ref, *rest):
    lagged, (mixed_ref, spec_ref) = rest[:-2], rest[-2:]
    copies, width, positions = mixed_ref.shape
    period = fwd_ref.shape[1] // 2
    terms = jnp.sum(terms_ref[...].astype(jnp.float32), axis=0)
    square = terms[3 * width : 3 * width + 1] + terms[3 * width + 1 : 3 * width + 2]
    gates = terms[: 3 * width] * lax.rsqrt(square * (1.0 / features) + 1e-06)
    live = lax.broadcasted_iota(jnp.int32, (1, positions), 1) < length_ref[0]
    driven = jnp.where(live, gates[width : 2 * width] * gates[:width], 0.0)
    spectrum = jnp.dot(driven.astype(jnp.bfloat16), fwd_ref[...], preferred_element_type=jnp.float32)
    real, imag = spectrum[:, :period], spectrum[:, period:]
    spec_ref[0] = real
    spec_ref[1] = imag
    zreal = filt_ref[0, 0] * real - filt_ref[0, 1] * imag
    zimag = filt_ref[0, 0] * imag + filt_ref[0, 1] * real
    for lag in range(1, past + 1):
        ref = lagged[lag - 1]
        zreal += filt_ref[lag, 0] * ref[0] - filt_ref[lag, 1] * ref[1]
        zimag += filt_ref[lag, 0] * ref[1] + filt_ref[lag, 1] * ref[0]
    if stored is not None:
        zreal += lagged[-1][stored, 0]
        zimag += lagged[-1][stored, 1]
    packed = jnp.concatenate([zreal, zimag], axis=1).astype(jnp.bfloat16)
    conv = jnp.dot(packed, inv_ref[...], preferred_element_type=jnp.float32)
    mixed = (gates[2 * width :] * (conv + skip_ref[...] * driven)).astype(mixed_ref.dtype)
    for y in range(copies):
        mixed_ref[y] = mixed


def emit_terms_kernel(x_ref, mixed_ref, *refs):
    blocks, out_ref = refs[:-1], refs[-1]
    groups, rows, _ = out_ref.shape
    mixed = mixed_ref[...]
    for step, block in enumerate(blocks):
        x = lax.rem(x_ref[0] + groups - step, groups)
        w = block[block.shape[0] - rows :]
        out_ref[x] = jnp.dot(w, mixed, preferred_element_type=jnp.float32).astype(out_ref.dtype)


def total_of(terms_ref, own_ref):
    total = own_ref[...].astype(jnp.float32) + jnp.sum(terms_ref[...].astype(jnp.float32), axis=0)
    return total.astype(own_ref.dtype)


def add_and_send_kernel(last_ref, terms_ref, own_ref, fresh_ref, out_ref, send_ref):
    out = total_of(terms_ref, own_ref)
    out_ref[...] = out
    send_ref[...] = jnp.where(last_ref[0] == 1, fresh_ref[...], out)


def finish_kernel(terms_ref, own_ref, *refs):
    earlier, out_ref = refs[:-1], refs[-1]
    for tick, ref in enumerate(earlier):
        out_ref[tick] = ref[...]
    out_ref[len(earlier)] = total_of(terms_ref, own_ref)


def local(feeds, newcomers, occupied, gain, value_w, in_w, out_w, emit_w, skip, filters, archive):
    section = lax.axis_index(SECTION)
    layers = lax.axis_size(SECTION)
    groups, copies = lax.axis_size("x"), lax.axis_size("y")
    ticks = newcomers.shape[0] + 1
    blocks = archive.shape[1]
    positions, width = feeds.shape[1:]
    features = gain.shape[1]
    rows = features // groups
    bf16 = functools.partial(jax.ShapeDtypeStruct, dtype=jnp.bfloat16)
    f32 = functools.partial(jax.ShapeDtypeStruct, dtype=jnp.float32)
    x = lax.axis_index("x").astype(jnp.int32)[None]
    last = (section == layers - 1).astype(jnp.int32)[None]
    lengths = [lax.dynamic_slice_in_dim(occupied, tick - section + layers - 1, 1, 0) for tick in range(ticks)]

    own = feeds[0].T
    part = gather_rows(jnp.broadcast_to(own[None], (copies,) + own.shape))
    dealt = call(
        deal_kernel,
        [bf16((4 * width, rows))] * groups,
        [x, gain] + [w[0].T for w in (value_w, in_w, out_w, emit_w)],
        "deal",
        smem=1,
    )
    weights = [dealt[0]] + [
        lax.ppermute(dealt[step], "x", [(i, (i + step) % groups) for i in range(groups)]) for step in range(1, groups)
    ]
    known, filters, forward, inverse = call(
        history_kernel,
        [f32((blocks,) + filters.shape[2:]), f32(filters.shape[1:])] + [bf16(t.shape) for t in tables(positions, filters.shape[-1])],
        [filters[0], archive[0]] + [jnp.asarray(t) for t in tables(positions, filters.shape[-1])],
        "history",
    )
    skip_column = skip[0][:, None]
    fresh = newcomers.transpose(0, 2, 1)

    ring = [(i, (i + 1) % layers) for i in range(layers)]
    outputs, spectra = [], []
    for tick in range(ticks):
        terms = call(
            gate_terms_kernel,
            bf16((groups, 3 * width + EXTRA, positions)),
            [x, part] + weights,
            "gate_terms",
            smem=1,
        )
        terms = swap(terms, "x")
        past = min(tick, blocks)
        stored = tick if tick < blocks else None
        lagged = spectra[::-1][:past] + ([known] if stored is not None else [])
        mixed, spectrum = call(
            functools.partial(mix_kernel, past, stored, features),
            [bf16((copies, width, positions)), f32((2, width, filters.shape[-1]))],
            [lengths[tick], terms, forward, inverse, filters, skip_column] + lagged,
            "mix",
            smem=1,
        )
        spectra.append(spectrum)
        terms = call(
            emit_terms_kernel,
            bf16((groups, width, positions)),
            [x, gather_rows(mixed)] + weights,
            "emit_terms",
            smem=1,
        )
        terms = swap(terms, "x")
        if tick < ticks - 1:
            out, send = call(
                add_and_send_kernel, [bf16(own.shape)] * 2, [last, terms, own, fresh[tick]], "add", smem=1
            )
            outputs.append(out)
            own = lax.ppermute(send, SECTION, ring)
            part = gather_rows(jnp.broadcast_to(own[None], (copies,) + own.shape))
    layer_out = call(finish_kernel, bf16((ticks,) + own.shape), [terms, own] + outputs, "finish")
    return layer_out.transpose(0, 2, 1)[None]


def solution(mesh):
    grid = Mesh(mesh.devices.reshape(8, 2, 4, 8), ("z", "core", "x", "y"))
    chan = ("x", "y")
    return jax.shard_map(
        local,
        mesh=grid,
        in_specs=(
            P(SECTION, None, chan),
            P(None, None, chan),
            P(),
            P(SECTION, None),
            P(SECTION, None, chan),
            P(SECTION, None, chan),
            P(SECTION, None, chan),
            P(SECTION, None, chan),
            P(SECTION, chan),
            P(SECTION, None, None, chan, None),
            P(SECTION, None, None, chan, None),
        ),
        out_specs=P(SECTION, None, None, chan),
        check_vma=False,
    )
```

```python
import functools

import jax
import jax.numpy as jnp
import numpy as np
from jax import lax
from jax.experimental import pallas as pl
from jax.experimental.pallas import tpu as pltpu
from jax.sharding import Mesh
from jax.sharding import PartitionSpec as P

SECTION = ("z", "core")
EXTRA = 16


def call(body, out, operands, name, smem=0):
    vmem = pl.BlockSpec(memory_space=pltpu.VMEM)
    scalars = pl.BlockSpec(memory_space=pltpu.SMEM)
    return pl.pallas_call(
        body,
        out_shape=out,
        in_specs=[scalars] * smem + [vmem] * (len(operands) - smem),
        out_specs=jax.tree.map(lambda _: vmem, out),
        compiler_params=pltpu.CompilerParams(vmem_limit_bytes=16 * 1024 * 1024),
        name=name,
    )(*operands)


def tables(length, period):
    half = period // 2
    phase = np.arange(length)[:, None] * np.arange(half)[None, :] % period
    cos, sin = np.cos(phase * (2.0 * np.pi / period)), -np.sin(phase * (2.0 * np.pi / period))
    sin[:, 0] = 1 - 2 * (np.arange(length) % 2)
    forward = np.concatenate([cos, sin], axis=1)
    weight = np.full((2 * half, 1), 2.0 / period)
    weight[0] = weight[half] = 1.0 / period
    return forward.astype(jnp.bfloat16), (forward.T * weight).astype(jnp.bfloat16)


def fold(full):
    half = full.shape[-1] // 2
    lower, upper = full[..., :half], full[..., half:]
    at = [lax.broadcasted_iota(jnp.int32, (half, half), axis) for axis in (0, 1)]
    mirror = jnp.where(at[0] + at[1] == half, 1.0, 0.0)
    mirrored = jnp.dot(
        upper.reshape(-1, half), mirror, precision=lax.Precision.HIGHEST, preferred_element_type=jnp.float32
    ).reshape(upper.shape)
    first = lax.broadcasted_iota(jnp.int32, lower.shape[1:], 1) == 0
    real = jnp.where(first, lower[0], 0.5 * (lower[0] + mirrored[0]))
    imag = jnp.where(first, upper[0], 0.5 * (lower[1] - mirrored[1]))
    return real, imag


def times(filt, spectrum):
    first = lax.broadcasted_iota(jnp.int32, filt[0].shape, 1) == 0
    imag = jnp.where(first, 0.0, filt[1])
    other = jnp.where(first, filt[1], filt[0])
    return filt[0] * spectrum[0] - imag * spectrum[1], other * spectrum[1] + imag * spectrum[0]


def swap(blocks, axis):
    return lax.all_to_all(blocks, axis, 0, 0, tiled=True)


def gather_rows(copies):
    got = swap(copies, "y")
    return got.reshape((-1, got.shape[-1]))


def deal_kernel(x_ref, gain_ref, *refs):
    matrices, blocks = refs[: len(refs) // 2], refs[len(refs) // 2 :]
    groups = len(blocks)
    width = matrices[0].shape[0]
    rows = blocks[0].shape[1]
    for step, block in enumerate(blocks):
        start = lax.rem(x_ref[0] + step, groups) * rows
        at = pl.ds(pl.multiple_of(start, rows), rows)
        gain = gain_ref[:, at]
        for m, matrix in enumerate(matrices):
            w = matrix[:, at]
            if m < len(matrices) - 1:
                w = (w.astype(jnp.float32) * gain).astype(w.dtype)
            block[m * width : (m + 1) * width] = w


def history_kernel(section_ref, lengths_ref, skip_ref, filt_ref, held_ref, *rest):
    passed, (live_ref, known_ref, filt_out, *handed) = rest[: (len(rest) - 3) // 2], rest[(len(rest) - 3) // 2 :]
    ticks, _, positions = live_ref.shape
    layers = lengths_ref.shape[0] - ticks + 1
    at = lax.broadcasted_iota(jnp.int32, (1, positions), 1)
    for tick in range(ticks):
        length = lengths_ref[tick - section_ref[0] + layers - 1]
        live_ref[tick] = jnp.where(at < length, 1.0, 0.0)
    blocks = held_ref.shape[0]
    for tick in range(blocks):
        real = imag = 0.0
        for lag in range(tick + 1, blocks + 1):
            first, second = held_ref[lag - tick - 1, 0], held_ref[lag - tick - 1, 1]
            real += filt_ref[lag, 0] * first - filt_ref[lag, 1] * second
            imag += filt_ref[lag, 0] * second + filt_ref[lag, 1] * first
        known_ref[tick, 0], known_ref[tick, 1] = fold(jnp.stack([real, imag]))
    for lag in range(blocks + 1):
        real, imag = fold(filt_ref[lag])
        if lag == 0:
            real += skip_ref[...]
            imag += jnp.where(lax.broadcasted_iota(jnp.int32, imag.shape, 1) == 0, skip_ref[...], 0.0)
        filt_out[lag, 0], filt_out[lag, 1] = real, imag
    for source, target in zip(passed, handed, strict=True):
        target[...] = source[...]


def gate_terms_kernel(x_ref, u_ref, *refs):
    out_ref = refs[-1]
    groups, rows, positions = out_ref.shape
    blocks = refs[:groups]
    rows -= EXTRA
    u = u_ref[...]
    wide = u.astype(jnp.float32)
    square = jnp.sum(wide * wide, axis=0, keepdims=True)
    upper = square.astype(jnp.bfloat16).astype(jnp.float32)
    at = lax.broadcasted_iota(jnp.int32, (EXTRA, positions), 0)
    extra = jnp.where(at == 0, upper, jnp.where(at == 1, square - upper, 0.0)).astype(out_ref.dtype)
    for step, block in enumerate(blocks):
        x = lax.rem(x_ref[0] + groups - step, groups)
        term = jnp.dot(block[:rows], u, preferred_element_type=jnp.float32)
        out_ref[x, :rows] = term.astype(out_ref.dtype)
        out_ref[x, rows:] = extra


def mix_kernel(tick, past, stored, features, live_ref, terms_ref, fwd_ref, inv_ref, filt_ref, *rest):
    lagged, (mixed_ref, spec_ref) = rest[:-2], rest[-2:]
    copies, width, _ = mixed_ref.shape
    half = fwd_ref.shape[1] // 2
    terms = jnp.sum(terms_ref[...].astype(jnp.float32), axis=0)
    square = terms[3 * width : 3 * width + 1] + terms[3 * width + 1 : 3 * width + 2]
    gates = terms[: 3 * width] * lax.rsqrt(square * (1.0 / features) + 1e-06)
    driven = jnp.where(live_ref[tick] > 0.0, gates[width : 2 * width] * gates[:width], 0.0)
    spectrum = jnp.dot(driven.astype(jnp.bfloat16), fwd_ref[...], preferred_element_type=jnp.float32)
    spectrum = spectrum[:, :half], spectrum[:, half:]
    spec_ref[0], spec_ref[1] = spectrum
    real, imag = times(filt_ref[0], spectrum)
    for lag in range(1, past + 1):
        more = times(filt_ref[lag], lagged[lag - 1][...])
        real, imag = real + more[0], imag + more[1]
    if stored is not None:
        real, imag = real + lagged[-1][stored, 0], imag + lagged[-1][stored, 1]
    packed = jnp.concatenate([real, imag], axis=1).astype(jnp.bfloat16)
    conv = jnp.dot(packed, inv_ref[...], preferred_element_type=jnp.float32)
    mixed = (gates[2 * width :] * conv).astype(mixed_ref.dtype)
    for y in range(copies):
        mixed_ref[y] = mixed


def emit_terms_kernel(x_ref, mixed_ref, *refs):
    blocks, out_ref = refs[:-1], refs[-1]
    groups, rows, _ = out_ref.shape
    mixed = mixed_ref[...]
    for step, block in enumerate(blocks):
        x = lax.rem(x_ref[0] + groups - step, groups)
        w = block[block.shape[0] - rows :]
        out_ref[x] = jnp.dot(w, mixed, preferred_element_type=jnp.float32).astype(out_ref.dtype)


def total_of(terms_ref, own_ref):
    total = own_ref[...].astype(jnp.float32) + jnp.sum(terms_ref[...].astype(jnp.float32), axis=0)
    return total.astype(own_ref.dtype)


def add_and_send_kernel(tick, last_ref, terms_ref, own_ref, fresh_ref, out_ref, send_ref):
    out = total_of(terms_ref, own_ref)
    out_ref[...] = out
    send_ref[...] = jnp.where(last_ref[0] == 1, fresh_ref[tick], out)


def finish_kernel(terms_ref, own_ref, *refs):
    earlier, out_ref = refs[:-1], refs[-1]
    for tick, ref in enumerate(earlier):
        out_ref[tick] = ref[...]
    out_ref[len(earlier)] = total_of(terms_ref, own_ref)


def local(feeds, newcomers, occupied, gain, value_w, in_w, out_w, emit_w, skip, filters, archive):
    section = lax.axis_index(SECTION)
    layers = lax.axis_size(SECTION)
    groups, copies = lax.axis_size("x"), lax.axis_size("y")
    ticks = newcomers.shape[0] + 1
    blocks = archive.shape[1]
    positions, width = feeds.shape[1:]
    features = gain.shape[1]
    rows = features // groups
    bf16 = functools.partial(jax.ShapeDtypeStruct, dtype=jnp.bfloat16)
    f32 = functools.partial(jax.ShapeDtypeStruct, dtype=jnp.float32)
    x = lax.axis_index("x").astype(jnp.int32)[None]
    last = (section == layers - 1).astype(jnp.int32)[None]

    own = feeds[0].T
    part = gather_rows(jnp.broadcast_to(own[None], (copies,) + own.shape))
    dealt = call(
        deal_kernel,
        [bf16((4 * width, rows))] * groups,
        [x, gain] + [w[0].T for w in (value_w, in_w, out_w, emit_w)],
        "deal",
        smem=1,
    )
    weights = [dealt[0]] + [None] * (groups - 1)
    for step in sorted(range(1, groups), key=lambda step: -min(step, groups - step)):
        pairs = [(i, (i + step) % groups) for i in range(groups)]
        weights[step] = lax.ppermute(dealt[step], "x", pairs)
    half = filters.shape[-1] // 2
    passed = [jnp.asarray(t) for t in tables(positions, 2 * half)] + [newcomers.transpose(0, 2, 1), own]
    live, known, filters, forward, inverse, fresh, own = call(
        history_kernel,
        [f32((ticks, 1, positions)), f32((blocks, 2, width, half)), f32((blocks + 1, 2, width, half))]
        + [jax.ShapeDtypeStruct(t.shape, t.dtype) for t in passed],
        [section.astype(jnp.int32)[None], occupied, skip[0][:, None], filters[0], archive[0]] + passed,
        "history",
        smem=2,
    )

    ring = [(i, (i + 1) % layers) for i in range(layers)]
    outputs, spectra = [], []
    for tick in range(ticks):
        terms = call(
            gate_terms_kernel,
            bf16((groups, 3 * width + EXTRA, positions)),
            [x, part] + weights + ([live] if tick == 0 else []),
            "gate_terms",
            smem=1,
        )
        terms = swap(terms, "x")
        past = min(tick, blocks)
        stored = tick if tick < blocks else None
        lagged = spectra[::-1][:past] + ([known] if stored is not None else [])
        mixed, spectrum = call(
            functools.partial(mix_kernel, tick, past, stored, features),
            [bf16((copies, width, positions)), f32((2, width, half))],
            [live, terms, forward, inverse, filters] + lagged,
            "mix",
        )
        spectra.append(spectrum)
        terms = call(
            emit_terms_kernel,
            bf16((groups, width, positions)),
            [x, gather_rows(mixed)] + weights,
            "emit_terms",
            smem=1,
        )
        terms = swap(terms, "x")
        if tick < ticks - 1:
            out, send = call(
                functools.partial(add_and_send_kernel, tick),
                [bf16(own.shape)] * 2,
                [last, terms, own, fresh],
                "add",
                smem=1,
            )
            outputs.append(out)
            own = lax.ppermute(send, SECTION, ring)
            part = gather_rows(jnp.broadcast_to(own[None], (copies,) + own.shape))
    layer_out = call(finish_kernel, bf16((ticks,) + own.shape), [terms, own] + outputs, "finish")
    return layer_out.transpose(0, 2, 1)[None]


def solution(mesh):
    grid = Mesh(mesh.devices.reshape(8, 2, 4, 8), ("z", "core", "x", "y"))
    chan = ("x", "y")
    return jax.shard_map(
        local,
        mesh=grid,
        in_specs=(
            P(SECTION, None, chan),
            P(None, None, chan),
            P(),
            P(SECTION, None),
            P(SECTION, None, chan),
            P(SECTION, None, chan),
            P(SECTION, None, chan),
            P(SECTION, None, chan),
            P(SECTION, chan),
            P(SECTION, None, None, chan, None),
            P(SECTION, None, None, chan, None),
        ),
        out_specs=P(SECTION, None, None, chan),
        check_vma=False,
    )
```

```python
import functools

import jax
import jax.numpy as jnp
import numpy as np
from jax import lax
from jax.experimental import pallas as pl
from jax.experimental.pallas import tpu as pltpu
from jax.sharding import Mesh
from jax.sharding import PartitionSpec as P

SECTION = ("z", "core")
EXTRA = 16


def call(body, out, operands, name, smem=0):
    vmem = pl.BlockSpec(memory_space=pltpu.VMEM)
    scalars = pl.BlockSpec(memory_space=pltpu.SMEM)
    return pl.pallas_call(
        body,
        out_shape=out,
        in_specs=[scalars] * smem + [vmem] * (len(operands) - smem),
        out_specs=jax.tree.map(lambda _: vmem, out),
        compiler_params=pltpu.CompilerParams(vmem_limit_bytes=16 * 1024 * 1024),
        name=name,
    )(*operands)


def tables(length, period):
    half = period // 2
    phase = np.arange(length)[:, None] * np.arange(half)[None, :] % period
    cos, sin = np.cos(phase * (2.0 * np.pi / period)), -np.sin(phase * (2.0 * np.pi / period))
    sin[:, 0] = 1 - 2 * (np.arange(length) % 2)
    forward = np.concatenate([cos, sin], axis=1)
    weight = np.full((2 * half, 1), 2.0 / period)
    weight[0] = weight[half] = 1.0 / period
    return forward.astype(jnp.bfloat16), (forward.T * weight).astype(jnp.bfloat16)


def fold(full):
    half = full.shape[-1] // 2
    lower, upper = full[..., :half], full[..., half:]
    at = [lax.broadcasted_iota(jnp.int32, (half, half), axis) for axis in (0, 1)]
    mirror = jnp.where(at[0] + at[1] == half, 1.0, 0.0)
    mirrored = jnp.dot(
        upper.reshape(-1, half), mirror, precision=lax.Precision.HIGHEST, preferred_element_type=jnp.float32
    ).reshape(upper.shape)
    first = lax.broadcasted_iota(jnp.int32, lower.shape[1:], 1) == 0
    real = jnp.where(first, lower[0], 0.5 * (lower[0] + mirrored[0]))
    imag = jnp.where(first, upper[0], 0.5 * (lower[1] - mirrored[1]))
    return real, imag


def times(filt, spectrum):
    first = lax.broadcasted_iota(jnp.int32, filt[0].shape, 1) == 0
    imag = jnp.where(first, 0.0, filt[1])
    other = jnp.where(first, filt[1], filt[0])
    return filt[0] * spectrum[0] - imag * spectrum[1], other * spectrum[1] + imag * spectrum[0]


def swap(blocks, axis):
    return lax.all_to_all(blocks, axis, 0, 0, tiled=True)


def gather_rows(copies):
    got = swap(copies, "y")
    return got.reshape((-1, got.shape[-1]))


def deal_kernel(x_ref, gain_ref, *refs):
    matrices, blocks = refs[: len(refs) // 2], refs[len(refs) // 2 :]
    groups = len(blocks)
    width = matrices[0].shape[0]
    rows = blocks[0].shape[1]
    for step, block in enumerate(blocks):
        start = lax.rem(x_ref[0] + step, groups) * rows
        at = pl.ds(pl.multiple_of(start, rows), rows)
        gain = gain_ref[:, at]
        for m, matrix in enumerate(matrices):
            w = matrix[:, at]
            if m < len(matrices) - 1:
                w = (w.astype(jnp.float32) * gain).astype(w.dtype)
            block[m * width : (m + 1) * width] = w


def history_kernel(section_ref, lengths_ref, skip_ref, filt_ref, held_ref, *rest):
    passed, (live_ref, known_ref, filt_out, *handed) = rest[: (len(rest) - 3) // 2], rest[(len(rest) - 3) // 2 :]
    ticks, _, positions = live_ref.shape
    layers = lengths_ref.shape[0] - ticks + 1
    at = lax.broadcasted_iota(jnp.int32, (1, positions), 1)
    for tick in range(ticks):
        length = lengths_ref[tick - section_ref[0] + layers - 1]
        live_ref[tick] = jnp.where(at < length, 1.0, 0.0)
    blocks = held_ref.shape[0]
    for tick in range(blocks):
        real = imag = 0.0
        for lag in range(tick + 1, blocks + 1):
            first, second = held_ref[lag - tick - 1, 0], held_ref[lag - tick - 1, 1]
            real += filt_ref[lag, 0] * first - filt_ref[lag, 1] * second
            imag += filt_ref[lag, 0] * second + filt_ref[lag, 1] * first
        real, imag = fold(jnp.stack([real, imag]))
        known_ref[tick, 0], known_ref[tick, 1] = real.astype(known_ref.dtype), imag.astype(known_ref.dtype)
    for lag in range(blocks + 1):
        real, imag = fold(filt_ref[lag])
        if lag == 0:
            real += skip_ref[...]
            imag += jnp.where(lax.broadcasted_iota(jnp.int32, imag.shape, 1) == 0, skip_ref[...], 0.0)
        filt_out[lag, 0], filt_out[lag, 1] = real, imag
    for source, target in zip(passed, handed, strict=True):
        target[...] = source[...]


def gate_terms_kernel(x_ref, u_ref, *refs):
    out_ref = refs[-1]
    groups, rows, positions = out_ref.shape
    blocks = refs[:groups]
    rows -= EXTRA
    u = u_ref[...]
    wide = u.astype(jnp.float32)
    square = jnp.sum(wide * wide, axis=0, keepdims=True)
    upper = square.astype(jnp.bfloat16).astype(jnp.float32)
    at = lax.broadcasted_iota(jnp.int32, (EXTRA, positions), 0)
    extra = jnp.where(at == 0, upper, jnp.where(at == 1, square - upper, 0.0)).astype(out_ref.dtype)
    for step, block in enumerate(blocks):
        x = lax.rem(x_ref[0] + groups - step, groups)
        term = jnp.dot(block[:rows], u, preferred_element_type=jnp.float32)
        out_ref[x, :rows] = term.astype(out_ref.dtype)
        out_ref[x, rows:] = extra


def mix_kernel(tick, past, stored, features, live_ref, terms_ref, fwd_ref, inv_ref, filt_ref, *rest):
    count = past + (stored is not None)
    lagged, mixed_ref, spec_ref = rest[:count], rest[count], rest[count + 1 :]
    copies, width, _ = mixed_ref.shape
    half = fwd_ref.shape[1] // 2
    terms = jnp.sum(terms_ref[...].astype(jnp.float32), axis=0)
    square = terms[3 * width : 3 * width + 1] + terms[3 * width + 1 : 3 * width + 2]
    gates = terms[: 3 * width] * lax.rsqrt(square * (1.0 / features) + 1e-06)
    driven = jnp.where(live_ref[tick] > 0.0, gates[width : 2 * width] * gates[:width], 0.0)
    spectrum = jnp.dot(driven.astype(jnp.bfloat16), fwd_ref[...], preferred_element_type=jnp.float32)
    spectrum = spectrum[:, :half], spectrum[:, half:]
    for ref in spec_ref:
        ref[0], ref[1] = spectrum
    real, imag = times(filt_ref[0], spectrum)
    for lag in range(1, past + 1):
        more = times(filt_ref[lag], lagged[lag - 1][...])
        real, imag = real + more[0], imag + more[1]
    if stored is not None:
        more = lagged[-1][stored].astype(jnp.float32)
        real, imag = real + more[0], imag + more[1]
    packed = jnp.concatenate([real, imag], axis=1).astype(jnp.bfloat16)
    conv = jnp.dot(packed, inv_ref[...], preferred_element_type=jnp.float32)
    mixed = (gates[2 * width :] * conv).astype(mixed_ref.dtype)
    for y in range(copies):
        mixed_ref[y] = mixed


def emit_terms_kernel(x_ref, mixed_ref, *refs):
    blocks, out_ref = refs[:-1], refs[-1]
    groups, rows, _ = out_ref.shape
    mixed = mixed_ref[...]
    for step, block in enumerate(blocks):
        x = lax.rem(x_ref[0] + groups - step, groups)
        w = block[block.shape[0] - rows :]
        out_ref[x] = jnp.dot(w, mixed, preferred_element_type=jnp.float32).astype(out_ref.dtype)


def total_of(terms_ref, own_ref):
    total = own_ref[...].astype(jnp.float32) + jnp.sum(terms_ref[...].astype(jnp.float32), axis=0)
    return total.astype(own_ref.dtype)


def add_and_send_kernel(tick, layers, section_ref, terms_ref, own_ref, fresh_ref, out_ref, send_ref):
    out = total_of(terms_ref, own_ref)
    out_ref[...] = out
    send_ref[...] = jnp.where(section_ref[0] == layers - 1, fresh_ref[tick], out)


def finish_kernel(terms_ref, own_ref, *refs):
    earlier, out_ref = refs[:-1], refs[-1]
    for tick, ref in enumerate(earlier):
        out_ref[tick] = ref[...]
    out_ref[len(earlier)] = total_of(terms_ref, own_ref)


def local(feeds, newcomers, occupied, gain, value_w, in_w, out_w, emit_w, skip, filters, archive):
    section = lax.axis_index(SECTION)
    layers = lax.axis_size(SECTION)
    groups, copies = lax.axis_size("x"), lax.axis_size("y")
    ticks = newcomers.shape[0] + 1
    blocks = archive.shape[1]
    positions, width = feeds.shape[1:]
    features = gain.shape[1]
    rows = features // groups
    bf16 = functools.partial(jax.ShapeDtypeStruct, dtype=jnp.bfloat16)
    f32 = functools.partial(jax.ShapeDtypeStruct, dtype=jnp.float32)
    x = lax.axis_index("x").astype(jnp.int32)[None]
    place = section.astype(jnp.int32)[None]

    own = feeds[0].T
    part = gather_rows(jnp.broadcast_to(own[None], (copies,) + own.shape))
    dealt = call(
        deal_kernel,
        [bf16((4 * width, rows))] * groups,
        [x, gain] + [w[0].T for w in (value_w, in_w, out_w, emit_w)],
        "deal",
        smem=1,
    )
    weights = [dealt[0]] + [None] * (groups - 1)
    for step in sorted(range(1, groups), key=lambda step: -min(step, groups - step)):
        pairs = [(i, (i + step) % groups) for i in range(groups)]
        weights[step] = lax.ppermute(dealt[step], "x", pairs)
    half = filters.shape[-1] // 2
    passed = [jnp.asarray(t) for t in tables(positions, 2 * half)] + [newcomers.transpose(0, 2, 1), own]
    live, known, filters, forward, inverse, fresh, own = call(
        history_kernel,
        [f32((ticks, 1, positions)), bf16((blocks, 2, width, half)), f32((blocks + 1, 2, width, half))]
        + [jax.ShapeDtypeStruct(t.shape, t.dtype) for t in passed],
        [place, occupied, skip[0][:, None], filters[0], archive[0]] + passed,
        "history",
        smem=2,
    )

    ring = [(i, (i + 1) % layers) for i in range(layers)]
    outputs, spectra = [], []
    for tick in range(ticks):
        terms = call(
            gate_terms_kernel,
            bf16((groups, 3 * width + EXTRA, positions)),
            [x, part] + weights + ([live] if tick == 0 else []),
            "gate_terms",
            smem=1,
        )
        terms = swap(terms, "x")
        past = min(tick, blocks)
        stored = tick if tick < blocks else None
        lagged = spectra[::-1][:past] + ([known] if stored is not None else [])
        mixed, *spectrum = call(
            functools.partial(mix_kernel, tick, past, stored, features),
            [bf16((copies, width, positions))] + [f32((2, width, half))] * (tick < ticks - 1),
            [live, terms, forward, inverse, filters] + lagged,
            "mix",
        )
        spectra += spectrum
        terms = call(
            emit_terms_kernel,
            bf16((groups, width, positions)),
            [x, gather_rows(mixed)] + weights,
            "emit_terms",
            smem=1,
        )
        terms = swap(terms, "x")
        if tick < ticks - 1:
            out, send = call(
                functools.partial(add_and_send_kernel, tick, layers),
                [bf16(own.shape)] * 2,
                [place, terms, own, fresh],
                "add",
                smem=1,
            )
            outputs.append(out)
            own = lax.ppermute(send, SECTION, ring)
            part = gather_rows(jnp.broadcast_to(own[None], (copies,) + own.shape))
    layer_out = call(finish_kernel, bf16((ticks,) + own.shape), [terms, own] + outputs, "finish")
    return layer_out.transpose(0, 2, 1)[None]


def solution(mesh):
    grid = Mesh(mesh.devices.reshape(8, 2, 4, 8), ("z", "core", "x", "y"))
    chan = ("x", "y")
    return jax.shard_map(
        local,
        mesh=grid,
        in_specs=(
            P(SECTION, None, chan),
            P(None, None, chan),
            P(),
            P(SECTION, None),
            P(SECTION, None, chan),
            P(SECTION, None, chan),
            P(SECTION, None, chan),
            P(SECTION, None, chan),
            P(SECTION, chan),
            P(SECTION, None, None, chan, None),
            P(SECTION, None, None, chan, None),
        ),
        out_specs=P(SECTION, None, None, chan),
        check_vma=False,
    )
```

```python
import functools

import jax
import jax.numpy as jnp
import numpy as np
from jax import lax
from jax.experimental import pallas as pl
from jax.experimental.pallas import tpu as pltpu
from jax.sharding import Mesh
from jax.sharding import PartitionSpec as P

SECTION = ("z", "core")
EXTRA = 16


def call(body, out, operands, name, smem=0, after=0):
    vmem = pl.BlockSpec(memory_space=pltpu.VMEM)
    scalars = pl.BlockSpec(memory_space=pltpu.SMEM)
    return pl.pallas_call(
        body,
        out_shape=out,
        in_specs=[scalars] * smem
        + [vmem] * (len(operands) - smem - after)
        + [pl.BlockSpec(memory_space=pl.ANY)] * after,
        out_specs=jax.tree.map(lambda _: vmem, out),
        compiler_params=pltpu.CompilerParams(vmem_limit_bytes=16 * 1024 * 1024),
        name=name,
    )(*operands)


def tables(length, period):
    half = period // 2
    phase = np.arange(length)[:, None] * np.arange(half)[None, :] % period
    cos, sin = np.cos(phase * (2.0 * np.pi / period)), -np.sin(phase * (2.0 * np.pi / period))
    sin[:, 0] = 1 - 2 * (np.arange(length) % 2)
    forward = np.concatenate([cos, sin], axis=1)
    weight = np.full((2 * half, 1), 2.0 / period)
    weight[0] = weight[half] = 1.0 / period
    return forward.astype(jnp.bfloat16), (forward.T * weight).astype(jnp.bfloat16)


def fold(full):
    half = full.shape[-1] // 2
    lower, upper = full[..., :half], full[..., half:]
    at = [lax.broadcasted_iota(jnp.int32, (half, half), axis) for axis in (0, 1)]
    mirror = jnp.where(at[0] + at[1] == half, 1.0, 0.0)
    mirrored = jnp.dot(
        upper.reshape(-1, half), mirror, precision=lax.Precision.HIGHEST, preferred_element_type=jnp.float32
    ).reshape(upper.shape)
    first = lax.broadcasted_iota(jnp.int32, lower.shape[1:], 1) == 0
    real = jnp.where(first, lower[0], 0.5 * (lower[0] + mirrored[0]))
    imag = jnp.where(first, upper[0], 0.5 * (lower[1] - mirrored[1]))
    return real, imag


def times(filt, spectrum):
    first = lax.broadcasted_iota(jnp.int32, filt[0].shape, 1) == 0
    imag = jnp.where(first, 0.0, filt[1])
    other = jnp.where(first, filt[1], filt[0])
    return filt[0] * spectrum[0] - imag * spectrum[1], other * spectrum[1] + imag * spectrum[0]


def swap(blocks, axis):
    return lax.all_to_all(blocks, axis, 0, 0, tiled=True)


def gather_rows(copies):
    got = swap(copies, "y")
    return got.reshape((-1, got.shape[-1]))


def scaled(matrix_ref, gain_ref, at):
    return (matrix_ref[:, at].astype(jnp.float32) * gain_ref[:, at]).astype(matrix_ref.dtype)


def deal_kernel(x_ref, gain_ref, value_ref, in_ref, out_ref, _, *blocks):
    width, rows = value_ref.shape[0], blocks[0].shape[1]
    for step, block in enumerate(blocks):
        start = lax.rem(x_ref[0] + step, len(blocks)) * rows
        at = pl.ds(pl.multiple_of(start, rows), rows)
        for m, matrix in enumerate((value_ref, in_ref, out_ref)):
            block[m * width : (m + 1) * width] = scaled(matrix, gain_ref, at)


def pack_kernel(part_ref, emit_ref, _, out_ref):
    groups, size, positions = out_ref.shape
    rows, width = part_ref.shape[0], emit_ref.shape[0]
    for x in range(groups):
        out_ref[x, :rows] = part_ref[...]
        for piece in range((size - rows) // width):
            at = x * rows + piece * positions
            out_ref[x, rows + piece * width : rows + (piece + 1) * width] = emit_ref[:, at : at + positions]


def history_kernel(section_ref, lengths_ref, skip_ref, filt_ref, held_ref, *rest):
    passed, (live_ref, known_ref, filt_out, *handed) = rest[: (len(rest) - 3) // 2], rest[(len(rest) - 3) // 2 :]
    ticks, _, positions = live_ref.shape
    layers = lengths_ref.shape[0] - ticks + 1
    at = lax.broadcasted_iota(jnp.int32, (1, positions), 1)
    for tick in range(ticks):
        length = lengths_ref[tick - section_ref[0] + layers - 1]
        live_ref[tick] = jnp.where(at < length, 1.0, 0.0)
    blocks = held_ref.shape[0]
    for tick in range(blocks):
        real = imag = 0.0
        for lag in range(tick + 1, blocks + 1):
            first, second = held_ref[lag - tick - 1, 0], held_ref[lag - tick - 1, 1]
            real += filt_ref[lag, 0] * first - filt_ref[lag, 1] * second
            imag += filt_ref[lag, 0] * second + filt_ref[lag, 1] * first
        real, imag = fold(jnp.stack([real, imag]))
        known_ref[tick, 0], known_ref[tick, 1] = real.astype(known_ref.dtype), imag.astype(known_ref.dtype)
    for lag in range(blocks + 1):
        real, imag = fold(filt_ref[lag])
        if lag == 0:
            real += skip_ref[...]
            imag += jnp.where(lax.broadcasted_iota(jnp.int32, imag.shape, 1) == 0, skip_ref[...], 0.0)
        filt_out[lag, 0], filt_out[lag, 1] = real, imag
    for source, target in zip(passed, handed, strict=True):
        target[...] = source[...]


def gate_terms_kernel(x_ref, u_ref, *refs):
    out_ref = refs[-1]
    groups, rows, positions = out_ref.shape
    blocks = refs[:groups]
    rows -= EXTRA
    u = u_ref[...]
    wide = u.astype(jnp.float32)
    square = jnp.sum(wide * wide, axis=0, keepdims=True)
    upper = square.astype(jnp.bfloat16).astype(jnp.float32)
    at = lax.broadcasted_iota(jnp.int32, (EXTRA, positions), 0)
    extra = jnp.where(at == 0, upper, jnp.where(at == 1, square - upper, 0.0)).astype(out_ref.dtype)
    for step, block in enumerate(blocks):
        x = lax.rem(x_ref[0] + groups - step, groups)
        term = jnp.dot(block[...], u, preferred_element_type=jnp.float32)
        out_ref[x, :rows] = term.astype(out_ref.dtype)
        out_ref[x, rows:] = extra


def mix_of(gates, square, live, fwd_ref, inv_ref, filt_ref, lagged, stored, mixed_ref, spec_ref):
    copies, width, _ = mixed_ref.shape
    half = fwd_ref.shape[1] // 2
    gates = gates * lax.rsqrt(square + 1e-06)
    driven = jnp.where(live > 0.0, gates[width : 2 * width] * gates[:width], 0.0)
    spectrum = jnp.dot(driven.astype(jnp.bfloat16), fwd_ref[...], preferred_element_type=jnp.float32)
    spectrum = spectrum[:, :half], spectrum[:, half:]
    for ref in spec_ref:
        ref[0], ref[1] = spectrum
    real, imag = times(filt_ref[0], spectrum)
    for lag, ref in enumerate(lagged, 1):
        more = times(filt_ref[lag], ref[...])
        real, imag = real + more[0], imag + more[1]
    if stored is not None:
        more = stored.astype(jnp.float32)
        real, imag = real + more[0], imag + more[1]
    packed = jnp.concatenate([real, imag], axis=1).astype(jnp.bfloat16)
    conv = jnp.dot(packed, inv_ref[...], preferred_element_type=jnp.float32)
    mixed = (gates[2 * width :] * conv).astype(mixed_ref.dtype)
    for y in range(copies):
        mixed_ref[y] = mixed


def first_mix_kernel(live_ref, packed_ref, gain_ref, value_ref, in_ref, out_ref, *rest):
    fwd_ref, inv_ref, filt_ref, known_ref, mixed_ref, spec_ref, emit_ref = rest
    groups = packed_ref.shape[0]
    rows = value_ref.shape[1] // groups
    width = value_ref.shape[0]
    gates = square = 0.0
    for x in range(groups):
        u = packed_ref[x, :rows]
        at = pl.ds(x * rows, rows)
        w = jnp.concatenate([scaled(m, gain_ref, at) for m in (value_ref, in_ref, out_ref)], axis=0)
        gates += jnp.dot(w, u, preferred_element_type=jnp.float32)
        wide = u.astype(jnp.float32)
        square += jnp.sum(wide * wide, axis=0, keepdims=True)
        for piece in range(emit_ref.shape[1]):
            emit_ref[x, piece] = packed_ref[x, rows + piece * width : rows + (piece + 1) * width]
    square = square * (1.0 / (groups * rows))
    mix_of(gates, square, live_ref[0], fwd_ref, inv_ref, filt_ref, (), known_ref[0], mixed_ref, (spec_ref,))


def mix_kernel(tick, past, stored, features, live_ref, terms_ref, fwd_ref, inv_ref, filt_ref, *rest):
    count = past + (stored is not None)
    lagged, mixed_ref, spec_ref = rest[:count], rest[count], rest[count + 1 :]
    width = mixed_ref.shape[1]
    terms = jnp.sum(terms_ref[...].astype(jnp.float32), axis=0)
    square = (terms[3 * width : 3 * width + 1] + terms[3 * width + 1 : 3 * width + 2]) * (1.0 / features)
    known = None if stored is None else lagged[-1][stored]
    mix_of(
        terms[: 3 * width], square, live_ref[tick], fwd_ref, inv_ref, filt_ref, lagged[:past], known, mixed_ref, spec_ref
    )


def emit_terms_kernel(w_ref, mixed_ref, out_ref):
    groups, pieces, _, size = w_ref.shape
    for x in range(groups):
        term = 0.0
        for piece in range(pieces):
            rows = mixed_ref[piece * size : (piece + 1) * size]
            term += jnp.dot(w_ref[x, piece], rows, preferred_element_type=jnp.float32)
        out_ref[x] = term.astype(out_ref.dtype)


def total_of(terms_ref, own_ref):
    total = own_ref[...].astype(jnp.float32) + jnp.sum(terms_ref[...].astype(jnp.float32), axis=0)
    return total.astype(own_ref.dtype)


def add_and_send_kernel(tick, layers, section_ref, terms_ref, own_ref, fresh_ref, *rest):
    out_ref, send_ref = rest[-2:]
    out = total_of(terms_ref, own_ref)
    out_ref[...] = out
    send_ref[...] = jnp.where(section_ref[0] == layers - 1, fresh_ref[tick], out)


def finish_kernel(terms_ref, own_ref, *refs):
    earlier, out_ref = refs[:-1], refs[-1]
    for tick, ref in enumerate(earlier):
        out_ref[tick] = ref[...]
    out_ref[len(earlier)] = total_of(terms_ref, own_ref)


def local(feeds, newcomers, occupied, gain, value_w, in_w, out_w, emit_w, skip, filters, archive):
    section = lax.axis_index(SECTION)
    layers = lax.axis_size(SECTION)
    groups, copies = lax.axis_size("x"), lax.axis_size("y")
    ticks = newcomers.shape[0] + 1
    blocks = archive.shape[1]
    positions, width = feeds.shape[1:]
    features = gain.shape[1]
    rows = features // groups
    bf16 = functools.partial(jax.ShapeDtypeStruct, dtype=jnp.bfloat16)
    f32 = functools.partial(jax.ShapeDtypeStruct, dtype=jnp.float32)
    x = lax.axis_index("x").astype(jnp.int32)[None]
    place = section.astype(jnp.int32)[None]

    own = feeds[0].T
    part = gather_rows(jnp.broadcast_to(own[None], (copies,) + own.shape))
    gate_w = [w[0].T for w in (value_w, in_w, out_w)]
    half = filters.shape[-1] // 2
    passed = [jnp.asarray(t) for t in tables(positions, 2 * half)] + [newcomers.transpose(0, 2, 1), own]
    live, known, filters, forward, inverse, fresh, own = call(
        history_kernel,
        [f32((ticks, 1, positions)), bf16((blocks, 2, width, half)), f32((blocks + 1, 2, width, half))]
        + [jax.ShapeDtypeStruct(t.shape, t.dtype) for t in passed],
        [place, occupied, skip[0][:, None], filters[0], archive[0]] + passed,
        "history",
        smem=2,
    )

    size = rows + width * rows // positions
    packed = swap(call(pack_kernel, bf16((groups, size, positions)), [part, emit_w[0].T, live], "pack"), "x")
    mixed, spectrum, emit_rows = call(
        first_mix_kernel,
        [bf16((copies, width, positions)), f32((2, width, half)), bf16((groups, rows // positions, width, positions))],
        [live, packed, gain] + gate_w + [forward, inverse, filters, known],
        "first_mix",
    )
    spectra = [spectrum]
    dealt = call(
        deal_kernel, [bf16((3 * width, rows))] * groups, [x, gain] + gate_w + [spectrum], "deal", smem=1
    )
    weights = [dealt[0]] + [
        lax.ppermute(dealt[step], "x", [(i, (i + step) % groups) for i in range(groups)]) for step in range(1, groups)
    ]

    ring = [(i, (i + 1) % layers) for i in range(layers)]
    outputs = []
    for tick in range(ticks):
        if tick > 0:
            terms = call(
                gate_terms_kernel,
                bf16((groups, 3 * width + EXTRA, positions)),
                [x, part] + weights,
                "gate_terms",
                smem=1,
            )
            terms = swap(terms, "x")
            past = min(tick, blocks)
            stored = tick if tick < blocks else None
            lagged = spectra[::-1][:past] + ([known] if stored is not None else [])
            mixed, *spectrum = call(
                functools.partial(mix_kernel, tick, past, stored, features),
                [bf16((copies, width, positions))] + [f32((2, width, half))] * (tick < ticks - 1),
                [live, terms, forward, inverse, filters] + lagged,
                "mix",
            )
            spectra += spectrum
        terms = call(
            emit_terms_kernel, bf16((groups, width, positions)), [emit_rows, gather_rows(mixed)], "emit_terms"
        )
        terms = swap(terms, "x")
        if tick < ticks - 1:
            out, send = call(
                functools.partial(add_and_send_kernel, tick, layers),
                [bf16(own.shape)] * 2,
                [place, terms, own, fresh] + (weights if tick == 0 else []),
                "add",
                smem=1,
                after=len(weights) if tick == 0 else 0,
            )
            outputs.append(out)
            own = lax.ppermute(send, SECTION, ring)
            part = gather_rows(jnp.broadcast_to(own[None], (copies,) + own.shape))
    layer_out = call(finish_kernel, bf16((ticks,) + own.shape), [terms, own] + outputs, "finish")
    return layer_out.transpose(0, 2, 1)[None]


def solution(mesh):
    grid = Mesh(mesh.devices.reshape(8, 2, 4, 8), ("z", "core", "x", "y"))
    chan = ("x", "y")
    return jax.shard_map(
        local,
        mesh=grid,
        in_specs=(
            P(SECTION, None, chan),
            P(None, None, chan),
            P(),
            P(SECTION, None),
            P(SECTION, None, chan),
            P(SECTION, None, chan),
            P(SECTION, None, chan),
            P(SECTION, None, chan),
            P(SECTION, chan),
            P(SECTION, None, None, chan, None),
            P(SECTION, None, None, chan, None),
        ),
        out_specs=P(SECTION, None, None, chan),
        check_vma=False,
    )
```

```python
import functools

import jax
import jax.numpy as jnp
import numpy as np
from jax import lax
from jax.experimental import pallas as pl
from jax.experimental.pallas import tpu as pltpu
from jax.sharding import Mesh
from jax.sharding import PartitionSpec as P

SECTION = ("z", "core")
EXTRA = 16


def call(body, out, operands, name, smem=0, after=0):
    vmem = pl.BlockSpec(memory_space=pltpu.VMEM)
    scalars = pl.BlockSpec(memory_space=pltpu.SMEM)
    return pl.pallas_call(
        body,
        out_shape=out,
        in_specs=[scalars] * smem
        + [vmem] * (len(operands) - smem - after)
        + [pl.BlockSpec(memory_space=pl.ANY)] * after,
        out_specs=jax.tree.map(lambda _: vmem, out),
        compiler_params=pltpu.CompilerParams(vmem_limit_bytes=16 * 1024 * 1024),
        name=name,
    )(*operands)


def tables(length, period):
    half = period // 2
    phase = np.arange(length)[:, None] * np.arange(half)[None, :] % period
    cos, sin = np.cos(phase * (2.0 * np.pi / period)), -np.sin(phase * (2.0 * np.pi / period))
    sin[:, 0] = 1 - 2 * (np.arange(length) % 2)
    forward = np.concatenate([cos, sin], axis=1)
    weight = np.full((2 * half, 1), 2.0 / period)
    weight[0] = weight[half] = 1.0 / period
    inverse = forward.T * weight
    inverse = np.concatenate([inverse[:half], inverse[half:]], axis=1)
    return np.concatenate([forward, inverse], axis=0).astype(jnp.bfloat16)


def fold(full):
    half = full.shape[-1] // 2
    lower, upper = full[..., :half], full[..., half:]
    at = [lax.broadcasted_iota(jnp.int32, (half, half), axis) for axis in (0, 1)]
    mirror = jnp.where(at[0] + at[1] == half, 1.0, 0.0)
    mirrored = jnp.dot(
        upper.reshape(-1, half), mirror, precision=lax.Precision.HIGHEST, preferred_element_type=jnp.float32
    ).reshape(upper.shape)
    first = lax.broadcasted_iota(jnp.int32, lower.shape[1:], 1) == 0
    real = jnp.where(first, lower[0], 0.5 * (lower[0] + mirrored[0]))
    imag = jnp.where(first, upper[0], 0.5 * (lower[1] - mirrored[1]))
    return real, imag


def times(filt, spectrum):
    first = lax.broadcasted_iota(jnp.int32, filt[0].shape, 1) == 0
    imag = jnp.where(first, 0.0, filt[1])
    other = jnp.where(first, filt[1], filt[0])
    return filt[0] * spectrum[0] - imag * spectrum[1], other * spectrum[1] + imag * spectrum[0]


def swap(blocks, axis):
    return lax.all_to_all(blocks, axis, 0, 0, tiled=True)


def gather_rows(copies):
    got = swap(copies, "y")
    return got.reshape((-1, got.shape[-1]))


def scaled(matrix_ref, gain_ref, at):
    return (matrix_ref[:, at].astype(jnp.float32) * gain_ref[:, at]).astype(matrix_ref.dtype)


def deal_kernel(x_ref, gain_ref, value_ref, in_ref, out_ref, _, *blocks):
    width, rows = value_ref.shape[0], blocks[0].shape[1]
    for step, block in enumerate(blocks):
        start = lax.rem(x_ref[0] + step, len(blocks)) * rows
        at = pl.ds(pl.multiple_of(start, rows), rows)
        for m, matrix in enumerate((value_ref, in_ref, out_ref)):
            block[m * width : (m + 1) * width] = scaled(matrix, gain_ref, at)


def pack_kernel(part_ref, emit_ref, _, out_ref):
    groups, size, positions = out_ref.shape
    rows, width = part_ref.shape[0], emit_ref.shape[0]
    for x in range(groups):
        out_ref[x, :rows] = part_ref[...]
        for piece in range((size - rows) // width):
            at = x * rows + piece * positions
            out_ref[x, rows + piece * width : rows + (piece + 1) * width] = emit_ref[:, at : at + positions]


def history_kernel(section_ref, lengths_ref, skip_ref, filt_ref, held_ref, *rest):
    passed, (live_ref, known_ref, filt_out, *handed) = rest[: (len(rest) - 3) // 2], rest[(len(rest) - 3) // 2 :]
    ticks, _, positions = live_ref.shape
    layers = lengths_ref.shape[0] - ticks + 1
    at = lax.broadcasted_iota(jnp.int32, (1, positions), 1)
    for tick in range(ticks):
        length = lengths_ref[tick - section_ref[0] + layers - 1]
        live_ref[tick] = jnp.where(at < length, 1.0, 0.0)
    width = skip_ref.shape[1]
    diagonal = [lax.broadcasted_iota(jnp.int32, (width, width), axis) for axis in (0, 1)]
    skip = jnp.sum(jnp.where(diagonal[0] == diagonal[1], skip_ref[...], 0.0), axis=1, keepdims=True)
    blocks = held_ref.shape[0]
    for tick in range(blocks):
        real = imag = 0.0
        for lag in range(tick + 1, blocks + 1):
            first, second = held_ref[lag - tick - 1, 0], held_ref[lag - tick - 1, 1]
            real += filt_ref[lag, 0] * first - filt_ref[lag, 1] * second
            imag += filt_ref[lag, 0] * second + filt_ref[lag, 1] * first
        real, imag = fold(jnp.stack([real, imag]))
        known_ref[tick, 0], known_ref[tick, 1] = real.astype(known_ref.dtype), imag.astype(known_ref.dtype)
    for lag in range(blocks + 1):
        real, imag = fold(filt_ref[lag])
        if lag == 0:
            real += skip
            imag += jnp.where(lax.broadcasted_iota(jnp.int32, imag.shape, 1) == 0, skip, 0.0)
        filt_out[lag, 0], filt_out[lag, 1] = real, imag
    for source, target in zip(passed, handed, strict=True):
        target[...] = source[...]


def gate_terms_kernel(x_ref, u_ref, *refs):
    out_ref = refs[-1]
    groups, rows, positions = out_ref.shape
    blocks = refs[:groups]
    rows -= EXTRA
    u = u_ref[...]
    wide = u.astype(jnp.float32)
    square = jnp.sum(wide * wide, axis=0, keepdims=True)
    upper = square.astype(jnp.bfloat16).astype(jnp.float32)
    at = lax.broadcasted_iota(jnp.int32, (EXTRA, positions), 0)
    extra = jnp.where(at == 0, upper, jnp.where(at == 1, square - upper, 0.0)).astype(out_ref.dtype)
    for step, block in enumerate(blocks):
        x = lax.rem(x_ref[0] + groups - step, groups)
        term = jnp.dot(block[...], u, preferred_element_type=jnp.float32)
        out_ref[x, :rows] = term.astype(out_ref.dtype)
        out_ref[x, rows:] = extra


def mix_of(gates, square, live, table_ref, filt_ref, lagged, stored, mixed_ref, spec_ref):
    copies, width, positions = mixed_ref.shape
    half = table_ref.shape[1] // 2
    gates = gates * lax.rsqrt(square + 1e-06)
    driven = jnp.where(live > 0.0, gates[width : 2 * width] * gates[:width], 0.0)
    spectrum = jnp.dot(driven.astype(jnp.bfloat16), table_ref[:positions], preferred_element_type=jnp.float32)
    spectrum = spectrum[:, :half], spectrum[:, half:]
    for ref in spec_ref:
        ref[0], ref[1] = spectrum
    real, imag = times(filt_ref[0], spectrum)
    for lag, ref in enumerate(lagged, 1):
        more = times(filt_ref[lag], ref[...])
        real, imag = real + more[0], imag + more[1]
    if stored is not None:
        more = stored.astype(jnp.float32)
        real, imag = real + more[0], imag + more[1]
    inverse = table_ref[positions:]
    conv = jnp.dot(real.astype(jnp.bfloat16), inverse[:, :positions], preferred_element_type=jnp.float32)
    conv += jnp.dot(imag.astype(jnp.bfloat16), inverse[:, positions:], preferred_element_type=jnp.float32)
    mixed = (gates[2 * width :] * conv).astype(mixed_ref.dtype)
    for y in range(copies):
        mixed_ref[y] = mixed


def first_mix_kernel(live_ref, packed_ref, gain_ref, value_ref, in_ref, out_ref, *rest):
    table_ref, filt_ref, known_ref, mixed_ref, spec_ref, emit_ref = rest
    groups = packed_ref.shape[0]
    rows = value_ref.shape[1] // groups
    width = value_ref.shape[0]
    gates = square = 0.0
    for x in range(groups):
        u = packed_ref[x, :rows]
        at = pl.ds(x * rows, rows)
        w = jnp.concatenate([scaled(m, gain_ref, at) for m in (value_ref, in_ref, out_ref)], axis=0)
        gates += jnp.dot(w, u, preferred_element_type=jnp.float32)
        wide = u.astype(jnp.float32)
        square += jnp.sum(wide * wide, axis=0, keepdims=True)
        for piece in range(emit_ref.shape[1]):
            emit_ref[x, piece] = packed_ref[x, rows + piece * width : rows + (piece + 1) * width]
    square = square * (1.0 / (groups * rows))
    mix_of(gates, square, live_ref[0], table_ref, filt_ref, (), known_ref[0], mixed_ref, (spec_ref,))


def mix_kernel(tick, past, stored, features, live_ref, terms_ref, table_ref, filt_ref, *rest):
    count = past + (stored is not None)
    lagged, mixed_ref, spec_ref = rest[:count], rest[count], rest[count + 1 :]
    width = mixed_ref.shape[1]
    terms = jnp.sum(terms_ref[...].astype(jnp.float32), axis=0)
    square = (terms[3 * width : 3 * width + 1] + terms[3 * width + 1 : 3 * width + 2]) * (1.0 / features)
    known = None if stored is None else lagged[-1][stored]
    mix_of(
        terms[: 3 * width], square, live_ref[tick], table_ref, filt_ref, lagged[:past], known, mixed_ref, spec_ref
    )


def emit_terms_kernel(w_ref, mixed_ref, out_ref):
    groups, pieces, _, size = w_ref.shape
    for x in range(groups):
        term = 0.0
        for piece in range(pieces):
            rows = mixed_ref[piece * size : (piece + 1) * size]
            term += jnp.dot(w_ref[x, piece], rows, preferred_element_type=jnp.float32)
        out_ref[x] = term.astype(out_ref.dtype)


def total_of(terms_ref, own_ref):
    total = own_ref[...].astype(jnp.float32) + jnp.sum(terms_ref[...].astype(jnp.float32), axis=0)
    return total.astype(own_ref.dtype)


def add_and_send_kernel(tick, layers, section_ref, terms_ref, own_ref, fresh_ref, *rest):
    out_ref, send_ref = rest[-2:]
    out = total_of(terms_ref, own_ref)
    out_ref[...] = out
    send_ref[...] = jnp.where(section_ref[0] == layers - 1, fresh_ref[tick], out)


def finish_kernel(terms_ref, own_ref, *refs):
    earlier, out_ref = refs[:-1], refs[-1]
    for tick, ref in enumerate(earlier):
        out_ref[tick] = ref[...]
    out_ref[len(earlier)] = total_of(terms_ref, own_ref)


def local(feeds, newcomers, occupied, gain, value_w, in_w, out_w, emit_w, skip, filters, archive):
    section = lax.axis_index(SECTION)
    layers = lax.axis_size(SECTION)
    groups, copies = lax.axis_size("x"), lax.axis_size("y")
    ticks = newcomers.shape[0] + 1
    blocks = archive.shape[1]
    positions, width = feeds.shape[1:]
    features = gain.shape[1]
    rows = features // groups
    bf16 = functools.partial(jax.ShapeDtypeStruct, dtype=jnp.bfloat16)
    f32 = functools.partial(jax.ShapeDtypeStruct, dtype=jnp.float32)
    x = lax.axis_index("x").astype(jnp.int32)[None]
    place = section.astype(jnp.int32)[None]

    own = feeds[0].T
    part = gather_rows(jnp.broadcast_to(own[None], (copies,) + own.shape))
    gate_w = [w[0].T for w in (value_w, in_w, out_w)]
    half = filters.shape[-1] // 2
    fresh = newcomers.transpose(0, 2, 1)
    passed = [jnp.asarray(tables(positions, 2 * half)), fresh, own]
    live, known, filters, table, fresh, own = call(
        history_kernel,
        [f32((ticks, 1, positions)), bf16((blocks, 2, width, half)), f32((blocks + 1, 2, width, half))]
        + [jax.ShapeDtypeStruct(t.shape, t.dtype) for t in passed],
        [place, occupied, skip, filters[0], archive[0]] + passed,
        "history",
        smem=2,
    )

    size = rows + width * rows // positions
    packed = swap(call(pack_kernel, bf16((groups, size, positions)), [part, emit_w[0].T, live], "pack"), "x")
    mixed, spectrum, emit_rows = call(
        first_mix_kernel,
        [bf16((copies, width, positions)), f32((2, width, half)), bf16((groups, rows // positions, width, positions))],
        [live, packed, gain] + gate_w + [table, filters, known],
        "first_mix",
    )
    spectra = [spectrum]
    dealt = call(
        deal_kernel, [bf16((3 * width, rows))] * groups, [x, gain] + gate_w + [spectrum], "deal", smem=1
    )
    weights = [dealt[0]] + [
        lax.ppermute(dealt[step], "x", [(i, (i + step) % groups) for i in range(groups)]) for step in range(1, groups)
    ]

    ring = [(i, (i + 1) % layers) for i in range(layers)]
    outputs = []
    for tick in range(ticks):
        if tick > 0:
            terms = call(
                gate_terms_kernel,
                bf16((groups, 3 * width + EXTRA, positions)),
                [x, part] + weights,
                "gate_terms",
                smem=1,
            )
            terms = swap(terms, "x")
            past = min(tick, blocks)
            stored = tick if tick < blocks else None
            lagged = spectra[::-1][:past] + ([known] if stored is not None else [])
            mixed, *spectrum = call(
                functools.partial(mix_kernel, tick, past, stored, features),
                [bf16((copies, width, positions))] + [f32((2, width, half))] * (tick < ticks - 1),
                [live, terms, table, filters] + lagged,
                "mix",
            )
            spectra += spectrum
        terms = call(
            emit_terms_kernel, bf16((groups, width, positions)), [emit_rows, gather_rows(mixed)], "emit_terms"
        )
        terms = swap(terms, "x")
        if tick < ticks - 1:
            out, send = call(
                functools.partial(add_and_send_kernel, tick, layers),
                [bf16(own.shape)] * 2,
                [place, terms, own, fresh] + (weights if tick == 0 else []),
                "add",
                smem=1,
                after=len(weights) if tick == 0 else 0,
            )
            outputs.append(out)
            own = lax.ppermute(send, SECTION, ring)
            part = gather_rows(jnp.broadcast_to(own[None], (copies,) + own.shape))
    layer_out = call(finish_kernel, bf16((ticks,) + own.shape), [terms, own] + outputs, "finish")
    return layer_out.transpose(0, 2, 1)[None]


def solution(mesh):
    grid = Mesh(mesh.devices.reshape(8, 2, 4, 8), ("z", "core", "x", "y"))
    chan = ("x", "y")
    return jax.shard_map(
        local,
        mesh=grid,
        in_specs=(
            P(SECTION, None, chan),
            P(None, None, chan),
            P(),
            P(SECTION, None),
            P(SECTION, None, chan),
            P(SECTION, None, chan),
            P(SECTION, None, chan),
            P(SECTION, None, chan),
            P(SECTION, chan),
            P(SECTION, None, None, chan, None),
            P(SECTION, None, None, chan, None),
        ),
        out_specs=P(SECTION, None, None, chan),
        check_vma=False,
    )
```

```python
import functools

import jax
import jax.numpy as jnp
import numpy as np
from jax import lax
from jax.experimental import pallas as pl
from jax.experimental.pallas import tpu as pltpu
from jax.sharding import Mesh
from jax.sharding import PartitionSpec as P

SECTION = ("z", "core")
EXTRA = 16


def call(body, out, operands, name, smem=0, after=0):
    vmem = pl.BlockSpec(memory_space=pltpu.VMEM)
    scalars = pl.BlockSpec(memory_space=pltpu.SMEM)
    return pl.pallas_call(
        body,
        out_shape=out,
        in_specs=[scalars] * smem
        + [vmem] * (len(operands) - smem - after)
        + [pl.BlockSpec(memory_space=pl.ANY)] * after,
        out_specs=jax.tree.map(lambda _: vmem, out),
        compiler_params=pltpu.CompilerParams(vmem_limit_bytes=16 * 1024 * 1024),
        name=name,
    )(*operands)


def tables(length, period):
    half = period // 2
    phase = np.arange(length)[:, None] * np.arange(half)[None, :] % period
    cos, sin = np.cos(phase * (2.0 * np.pi / period)), -np.sin(phase * (2.0 * np.pi / period))
    sin[:, 0] = 1 - 2 * (np.arange(length) % 2)
    forward = np.concatenate([cos, sin], axis=1)
    weight = np.full((2 * half, 1), 2.0 / period)
    weight[0] = weight[half] = 1.0 / period
    inverse = forward.T * weight
    inverse = np.concatenate([inverse[:half], inverse[half:]], axis=1)
    return np.concatenate([forward, inverse], axis=0).astype(jnp.bfloat16)


def fold(full):
    half = full.shape[-1] // 2
    lower, upper = full[..., :half], full[..., half:]
    at = [lax.broadcasted_iota(jnp.int32, (half, half), axis) for axis in (0, 1)]
    mirror = jnp.where(at[0] + at[1] == half, 1.0, 0.0).astype(jnp.bfloat16)
    flat = upper.reshape(-1, half)
    high = flat.astype(jnp.bfloat16)
    low = (flat - high.astype(jnp.float32)).astype(jnp.bfloat16)
    mirrored = jnp.dot(high, mirror, preferred_element_type=jnp.float32)
    mirrored += jnp.dot(low, mirror, preferred_element_type=jnp.float32)
    mirrored = mirrored.reshape(upper.shape)
    first = lax.broadcasted_iota(jnp.int32, lower.shape[1:], 1) == 0
    real = jnp.where(first, lower[0], 0.5 * (lower[0] + mirrored[0]))
    imag = jnp.where(first, upper[0], 0.5 * (lower[1] - mirrored[1]))
    return real, imag


def times(filt, spectrum):
    first = lax.broadcasted_iota(jnp.int32, filt[0].shape, 1) == 0
    imag = jnp.where(first, 0.0, filt[1])
    other = jnp.where(first, filt[1], filt[0])
    return filt[0] * spectrum[0] - imag * spectrum[1], other * spectrum[1] + imag * spectrum[0]


def swap(blocks, axis):
    return lax.all_to_all(blocks, axis, 0, 0, tiled=True)


def gather_rows(copies):
    got = swap(copies, "y")
    return got.reshape((-1, got.shape[-1]))


def scaled(matrix_ref, gain_ref, at):
    return (matrix_ref[:, at].astype(jnp.float32) * gain_ref[:, at]).astype(matrix_ref.dtype)


def deal_kernel(x_ref, gain_ref, value_ref, in_ref, out_ref, _, *blocks):
    width, rows = value_ref.shape[0], blocks[0].shape[1]
    for step, block in enumerate(blocks):
        start = lax.rem(x_ref[0] + step, len(blocks)) * rows
        at = pl.ds(pl.multiple_of(start, rows), rows)
        for m, matrix in enumerate((value_ref, in_ref, out_ref)):
            block[m * width : (m + 1) * width] = scaled(matrix, gain_ref, at)


def pack_kernel(y_ref, part_ref, emit_ref, _, out_ref, own_ref):
    groups, size, positions = out_ref.shape
    at = pl.multiple_of(y_ref[0] * own_ref.shape[0], own_ref.shape[0])
    own_ref[...] = part_ref[pl.ds(at, own_ref.shape[0])]
    rows, width = part_ref.shape[0], emit_ref.shape[0]
    for x in range(groups):
        out_ref[x, :rows] = part_ref[...]
        for piece in range((size - rows) // width):
            at = x * rows + piece * positions
            out_ref[x, rows + piece * width : rows + (piece + 1) * width] = emit_ref[:, at : at + positions]


def history_kernel(section_ref, lengths_ref, skip_ref, filt_ref, held_ref, *rest):
    passed, (live_ref, known_ref, filt_out, *handed) = rest[: (len(rest) - 3) // 2], rest[(len(rest) - 3) // 2 :]
    ticks, _, positions = live_ref.shape
    layers = lengths_ref.shape[0] - ticks + 1
    at = lax.broadcasted_iota(jnp.int32, (1, positions), 1)
    for tick in range(ticks):
        length = lengths_ref[tick - section_ref[0] + layers - 1]
        live_ref[tick] = jnp.where(at < length, 1.0, 0.0)
    width = skip_ref.shape[1]
    diagonal = [lax.broadcasted_iota(jnp.int32, (width, width), axis) for axis in (0, 1)]
    skip = jnp.sum(jnp.where(diagonal[0] == diagonal[1], skip_ref[...], 0.0), axis=1, keepdims=True)
    blocks = held_ref.shape[0]
    for tick in range(blocks):
        real = imag = 0.0
        for lag in range(tick + 1, blocks + 1):
            first, second = held_ref[lag - tick - 1, 0], held_ref[lag - tick - 1, 1]
            real += filt_ref[lag, 0] * first - filt_ref[lag, 1] * second
            imag += filt_ref[lag, 0] * second + filt_ref[lag, 1] * first
        real, imag = fold(jnp.stack([real, imag]))
        known_ref[tick, 0], known_ref[tick, 1] = real.astype(known_ref.dtype), imag.astype(known_ref.dtype)
    for lag in range(blocks + 1):
        real, imag = fold(filt_ref[lag])
        if lag == 0:
            real += skip
            imag += jnp.where(lax.broadcasted_iota(jnp.int32, imag.shape, 1) == 0, skip, 0.0)
        filt_out[lag, 0], filt_out[lag, 1] = real, imag
    for source, target in zip(passed, handed, strict=True):
        target[...] = source[...]


def gate_terms_kernel(x_ref, u_ref, *refs):
    out_ref = refs[-1]
    groups, rows, positions = out_ref.shape
    blocks = refs[:groups]
    rows -= EXTRA
    u = u_ref[...]
    wide = u.astype(jnp.float32)
    square = jnp.sum(wide * wide, axis=0, keepdims=True)
    upper = square.astype(jnp.bfloat16).astype(jnp.float32)
    at = lax.broadcasted_iota(jnp.int32, (EXTRA, positions), 0)
    extra = jnp.where(at == 0, upper, jnp.where(at == 1, square - upper, 0.0)).astype(out_ref.dtype)
    for step, block in enumerate(blocks):
        x = lax.rem(x_ref[0] + groups - step, groups)
        term = jnp.dot(block[...], u, preferred_element_type=jnp.float32)
        out_ref[x, :rows] = term.astype(out_ref.dtype)
        out_ref[x, rows:] = extra


def mix_of(gates, square, live, table_ref, filt_ref, lagged, stored, mixed_ref, spec_ref):
    copies, width, positions = mixed_ref.shape
    half = table_ref.shape[1] // 2
    gates = gates * lax.rsqrt(square + 1e-06)
    driven = jnp.where(live > 0.0, gates[width : 2 * width] * gates[:width], 0.0)
    spectrum = jnp.dot(driven.astype(jnp.bfloat16), table_ref[:positions], preferred_element_type=jnp.float32)
    spectrum = spectrum[:, :half], spectrum[:, half:]
    for ref in spec_ref:
        ref[0], ref[1] = spectrum
    real, imag = times(filt_ref[0], spectrum)
    for lag, ref in enumerate(lagged, 1):
        more = times(filt_ref[lag], ref[...])
        real, imag = real + more[0], imag + more[1]
    if stored is not None:
        more = stored.astype(jnp.float32)
        real, imag = real + more[0], imag + more[1]
    inverse = table_ref[positions:]
    conv = jnp.dot(real.astype(jnp.bfloat16), inverse[:, :positions], preferred_element_type=jnp.float32)
    conv += jnp.dot(imag.astype(jnp.bfloat16), inverse[:, positions:], preferred_element_type=jnp.float32)
    mixed = (gates[2 * width :] * conv).astype(mixed_ref.dtype)
    for y in range(copies):
        mixed_ref[y] = mixed


def first_mix_kernel(live_ref, packed_ref, gain_ref, value_ref, in_ref, out_ref, *rest):
    table_ref, filt_ref, known_ref, mixed_ref, spec_ref, emit_ref = rest
    groups = packed_ref.shape[0]
    rows = value_ref.shape[1] // groups
    width = value_ref.shape[0]
    gates = square = 0.0
    for x in range(groups):
        u = packed_ref[x, :rows]
        at = pl.ds(x * rows, rows)
        w = jnp.concatenate([scaled(m, gain_ref, at) for m in (value_ref, in_ref, out_ref)], axis=0)
        gates += jnp.dot(w, u, preferred_element_type=jnp.float32)
        wide = u.astype(jnp.float32)
        square += jnp.sum(wide * wide, axis=0, keepdims=True)
        for piece in range(emit_ref.shape[1]):
            emit_ref[x, piece] = packed_ref[x, rows + piece * width : rows + (piece + 1) * width]
    square = square * (1.0 / (groups * rows))
    mix_of(gates, square, live_ref[0], table_ref, filt_ref, (), known_ref[0], mixed_ref, (spec_ref,))


def mix_kernel(tick, past, stored, features, live_ref, terms_ref, table_ref, filt_ref, *rest):
    count = past + (stored is not None)
    lagged, mixed_ref, spec_ref = rest[:count], rest[count], rest[count + 1 :]
    width = mixed_ref.shape[1]
    terms = jnp.sum(terms_ref[...].astype(jnp.float32), axis=0)
    square = (terms[3 * width : 3 * width + 1] + terms[3 * width + 1 : 3 * width + 2]) * (1.0 / features)
    known = None if stored is None else lagged[-1][stored]
    mix_of(
        terms[: 3 * width], square, live_ref[tick], table_ref, filt_ref, lagged[:past], known, mixed_ref, spec_ref
    )


def emit_terms_kernel(w_ref, mixed_ref, out_ref):
    groups, pieces, _, size = w_ref.shape
    for x in range(groups):
        term = 0.0
        for piece in range(pieces):
            rows = mixed_ref[piece * size : (piece + 1) * size]
            term += jnp.dot(w_ref[x, piece], rows, preferred_element_type=jnp.float32)
        out_ref[x] = term.astype(out_ref.dtype)


def total_of(terms_ref, own_ref):
    total = own_ref[...].astype(jnp.float32) + jnp.sum(terms_ref[...].astype(jnp.float32), axis=0)
    return total.astype(own_ref.dtype)


def spread_kernel(own_ref, *rest):
    for y in range(rest[-1].shape[0]):
        rest[-1][y] = own_ref[...]


def add_and_send_kernel(tick, layers, section_ref, terms_ref, own_ref, fresh_ref, out_ref, send_ref):
    out = total_of(terms_ref, own_ref)
    out_ref[...] = out
    send_ref[...] = jnp.where(section_ref[0] == layers - 1, fresh_ref[tick], out)


def finish_kernel(terms_ref, own_ref, *refs):
    earlier, out_ref = refs[:-1], refs[-1]
    for tick, ref in enumerate(earlier):
        out_ref[tick] = ref[...]
    out_ref[len(earlier)] = total_of(terms_ref, own_ref)


def local(feeds, newcomers, occupied, gain, value_w, in_w, out_w, emit_w, skip, filters, archive):
    section = lax.axis_index(SECTION)
    layers = lax.axis_size(SECTION)
    groups, copies = lax.axis_size("x"), lax.axis_size("y")
    ticks = newcomers.shape[0] + 1
    blocks = archive.shape[1]
    positions, width = feeds.shape[1:]
    features = gain.shape[1]
    rows = features // groups
    bf16 = functools.partial(jax.ShapeDtypeStruct, dtype=jnp.bfloat16)
    f32 = functools.partial(jax.ShapeDtypeStruct, dtype=jnp.float32)
    x = lax.axis_index("x").astype(jnp.int32)[None]
    place = section.astype(jnp.int32)[None]

    own = feeds[0].T
    part = gather_rows(jnp.broadcast_to(own[None], (copies,) + own.shape))
    gate_w = [w[0].T for w in (value_w, in_w, out_w)]
    half = filters.shape[-1] // 2
    fresh = newcomers.transpose(0, 2, 1)
    passed = [jnp.asarray(tables(positions, 2 * half)), fresh]
    live, known, filters, table, fresh = call(
        history_kernel,
        [f32((ticks, 1, positions)), bf16((blocks, 2, width, half)), f32((blocks + 1, 2, width, half))]
        + [jax.ShapeDtypeStruct(t.shape, t.dtype) for t in passed],
        [place, occupied, skip, filters[0], archive[0]] + passed,
        "history",
        smem=2,
    )

    size = rows + width * rows // positions
    packed, own = call(
        pack_kernel,
        [bf16((groups, size, positions)), bf16(own.shape)],
        [lax.axis_index("y").astype(jnp.int32)[None], part, emit_w[0].T, live],
        "pack",
        smem=1,
        after=1,
    )
    packed = swap(packed, "x")
    mixed, spectrum, emit_rows = call(
        first_mix_kernel,
        [bf16((copies, width, positions)), f32((2, width, half)), bf16((groups, rows // positions, width, positions))],
        [live, packed, gain] + gate_w + [table, filters, known],
        "first_mix",
    )
    spectra = [spectrum]
    dealt = call(
        deal_kernel, [bf16((3 * width, rows))] * groups, [x, gain] + gate_w + [spectrum], "deal", smem=1
    )
    weights = [dealt[0]] + [
        lax.ppermute(dealt[step], "x", [(i, (i + step) % groups) for i in range(groups)]) for step in range(1, groups)
    ]

    ring = [(i, (i + 1) % layers) for i in range(layers)]
    outputs = []
    for tick in range(ticks):
        if tick > 0:
            terms = call(
                gate_terms_kernel,
                bf16((groups, 3 * width + EXTRA, positions)),
                [x, part] + weights,
                "gate_terms",
                smem=1,
            )
            terms = swap(terms, "x")
            past = min(tick, blocks)
            stored = tick if tick < blocks else None
            lagged = spectra[::-1][:past] + ([known] if stored is not None else [])
            mixed, *spectrum = call(
                functools.partial(mix_kernel, tick, past, stored, features),
                [bf16((copies, width, positions))] + [f32((2, width, half))] * (tick < ticks - 1),
                [live, terms, table, filters] + lagged,
                "mix",
            )
            spectra += spectrum
        terms = call(
            emit_terms_kernel, bf16((groups, width, positions)), [emit_rows, gather_rows(mixed)], "emit_terms"
        )
        terms = swap(terms, "x")
        if tick < ticks - 1:
            out, send = call(
                functools.partial(add_and_send_kernel, tick, layers),
                [bf16(own.shape)] * 2,
                [place, terms, own, fresh],
                "add",
                smem=1,
            )
            outputs.append(out)
            own = lax.ppermute(send, SECTION, ring)
            after = weights if tick == 0 else []
            spread = call(spread_kernel, bf16((copies,) + own.shape), [own] + after, "spread", after=len(after))
            part = gather_rows(spread)
    layer_out = call(finish_kernel, bf16((ticks,) + own.shape), [terms, own] + outputs, "finish")
    return layer_out.transpose(0, 2, 1)[None]


def solution(mesh):
    grid = Mesh(mesh.devices.reshape(8, 2, 4, 8), ("z", "core", "x", "y"))
    chan = ("x", "y")
    return jax.shard_map(
        local,
        mesh=grid,
        in_specs=(
            P(SECTION, None, chan),
            P(None, None, chan),
            P(),
            P(SECTION, None),
            P(SECTION, None, chan),
            P(SECTION, None, chan),
            P(SECTION, None, chan),
            P(SECTION, None, chan),
            P(SECTION, chan),
            P(SECTION, None, None, chan, None),
            P(SECTION, None, None, chan, None),
        ),
        out_specs=P(SECTION, None, None, chan),
        check_vma=False,
    )
```

```python
import functools

import jax
import jax.numpy as jnp
import numpy as np
from jax import lax
from jax.experimental import pallas as pl
from jax.experimental.pallas import tpu as pltpu
from jax.sharding import Mesh
from jax.sharding import PartitionSpec as P

SECTION = ("z", "core")
EXTRA = 16


def call(body, out, operands, name, smem=0, after=0):
    vmem = pl.BlockSpec(memory_space=pltpu.VMEM)
    scalars = pl.BlockSpec(memory_space=pltpu.SMEM)
    return pl.pallas_call(
        body,
        out_shape=out,
        in_specs=[scalars] * smem
        + [vmem] * (len(operands) - smem - after)
        + [pl.BlockSpec(memory_space=pl.ANY)] * after,
        out_specs=jax.tree.map(lambda _: vmem, out),
        compiler_params=pltpu.CompilerParams(vmem_limit_bytes=16 * 1024 * 1024),
        name=name,
    )(*operands)


def tables(length, period):
    half = period // 2
    phase = np.arange(length)[:, None] * np.arange(half)[None, :] % period
    cos, sin = np.cos(phase * (2.0 * np.pi / period)), -np.sin(phase * (2.0 * np.pi / period))
    sin[:, 0] = 1 - 2 * (np.arange(length) % 2)
    forward = np.concatenate([cos, sin], axis=1)
    weight = np.full((2 * half, 1), 2.0 / period)
    weight[0] = weight[half] = 1.0 / period
    inverse = forward.T * weight
    inverse = np.concatenate([inverse[:half], inverse[half:]], axis=1)
    return np.concatenate([forward, inverse], axis=0).astype(jnp.bfloat16)


def fold(full):
    half = full.shape[-1] // 2
    lower, upper = full[..., :half], full[..., half:]
    at = [lax.broadcasted_iota(jnp.int32, (half, half), axis) for axis in (0, 1)]
    mirror = jnp.where(at[0] + at[1] == half, 1.0, 0.0)
    mirrored = jnp.dot(
        upper.reshape(-1, half), mirror, precision=lax.Precision.HIGHEST, preferred_element_type=jnp.float32
    ).reshape(upper.shape)
    first = lax.broadcasted_iota(jnp.int32, lower.shape[1:], 1) == 0
    real = jnp.where(first, lower[0], 0.5 * (lower[0] + mirrored[0]))
    imag = jnp.where(first, upper[0], 0.5 * (lower[1] - mirrored[1]))
    return real, imag


def times(filt, spectrum):
    first = lax.broadcasted_iota(jnp.int32, filt[0].shape, 1) == 0
    imag = jnp.where(first, 0.0, filt[1])
    other = jnp.where(first, filt[1], filt[0])
    return filt[0] * spectrum[0] - imag * spectrum[1], other * spectrum[1] + imag * spectrum[0]


def swap(blocks, axis):
    return lax.all_to_all(blocks, axis, 0, 0, tiled=True)


def gather_rows(copies):
    got = swap(copies, "y")
    return got.reshape((-1, got.shape[-1]))


def scaled(matrix_ref, gain_ref, at):
    return (matrix_ref[:, at].astype(jnp.float32) * gain_ref[:, at]).astype(matrix_ref.dtype)


def deal_kernel(x_ref, gain_ref, value_ref, in_ref, out_ref, _, *blocks):
    width, rows = value_ref.shape[0], blocks[0].shape[1]
    for step, block in enumerate(blocks):
        start = lax.rem(x_ref[0] + step, len(blocks)) * rows
        at = pl.ds(pl.multiple_of(start, rows), rows)
        for m, matrix in enumerate((value_ref, in_ref, out_ref)):
            block[m * width : (m + 1) * width] = scaled(matrix, gain_ref, at)


def pack_kernel(part_ref, emit_ref, _, out_ref):
    groups, size, positions = out_ref.shape
    rows, width = part_ref.shape[0], emit_ref.shape[0]
    for x in range(groups):
        out_ref[x, :rows] = part_ref[...]
        for piece in range((size - rows) // width):
            at = x * rows + piece * positions
            out_ref[x, rows + piece * width : rows + (piece + 1) * width] = emit_ref[:, at : at + positions]


def history_kernel(section_ref, lengths_ref, skip_ref, filt_ref, held_ref, *rest):
    passed, (live_ref, known_ref, filt_out, *handed) = rest[: (len(rest) - 3) // 2], rest[(len(rest) - 3) // 2 :]
    ticks, _, positions = live_ref.shape
    layers = lengths_ref.shape[0] - ticks + 1
    at = lax.broadcasted_iota(jnp.int32, (1, positions), 1)
    for tick in range(ticks):
        length = lengths_ref[tick - section_ref[0] + layers - 1]
        live_ref[tick] = jnp.where(at < length, 1.0, 0.0)
    width = skip_ref.shape[1]
    diagonal = [lax.broadcasted_iota(jnp.int32, (width, width), axis) for axis in (0, 1)]
    skip = jnp.sum(jnp.where(diagonal[0] == diagonal[1], skip_ref[...], 0.0), axis=1, keepdims=True)
    blocks = held_ref.shape[0]
    for tick in range(blocks):
        real = imag = 0.0
        for lag in range(tick + 1, blocks + 1):
            first, second = held_ref[lag - tick - 1, 0], held_ref[lag - tick - 1, 1]
            real += filt_ref[lag, 0] * first - filt_ref[lag, 1] * second
            imag += filt_ref[lag, 0] * second + filt_ref[lag, 1] * first
        real, imag = fold(jnp.stack([real, imag]))
        known_ref[tick, 0], known_ref[tick, 1] = real.astype(known_ref.dtype), imag.astype(known_ref.dtype)
    for lag in range(blocks + 1):
        real, imag = fold(filt_ref[lag])
        if lag == 0:
            real += skip
            imag += jnp.where(lax.broadcasted_iota(jnp.int32, imag.shape, 1) == 0, skip, 0.0)
        filt_out[lag, 0], filt_out[lag, 1] = real, imag
    for source, target in zip(passed, handed, strict=True):
        target[...] = source[...]


def gate_terms_kernel(x_ref, u_ref, *refs):
    out_ref = refs[-1]
    groups, rows, positions = out_ref.shape
    blocks = refs[:groups]
    rows -= EXTRA
    u = u_ref[...]
    wide = u.astype(jnp.float32)
    square = jnp.sum(wide * wide, axis=0, keepdims=True)
    upper = square.astype(jnp.bfloat16).astype(jnp.float32)
    at = lax.broadcasted_iota(jnp.int32, (EXTRA, positions), 0)
    extra = jnp.where(at == 0, upper, jnp.where(at == 1, square - upper, 0.0)).astype(out_ref.dtype)
    for step, block in enumerate(blocks):
        x = lax.rem(x_ref[0] + groups - step, groups)
        term = jnp.dot(block[...], u, preferred_element_type=jnp.float32)
        out_ref[x, :rows] = term.astype(out_ref.dtype)
        out_ref[x, rows:] = extra


def mix_of(gates, square, live, table_ref, filt_ref, lagged, stored, mixed_ref, spec_ref):
    copies, width, positions = mixed_ref.shape
    half = table_ref.shape[1] // 2
    gates = gates * lax.rsqrt(square + 1e-06)
    driven = jnp.where(live > 0.0, gates[width : 2 * width] * gates[:width], 0.0)
    spectrum = jnp.dot(driven.astype(jnp.bfloat16), table_ref[:positions], preferred_element_type=jnp.float32)
    spectrum = spectrum[:, :half], spectrum[:, half:]
    for ref in spec_ref:
        ref[0], ref[1] = spectrum
    real, imag = times(filt_ref[0], spectrum)
    for lag, ref in enumerate(lagged, 1):
        more = times(filt_ref[lag], ref[...])
        real, imag = real + more[0], imag + more[1]
    if stored is not None:
        more = stored.astype(jnp.float32)
        real, imag = real + more[0], imag + more[1]
    inverse = table_ref[positions:]
    conv = jnp.dot(real.astype(jnp.bfloat16), inverse[:, :positions], preferred_element_type=jnp.float32)
    conv += jnp.dot(imag.astype(jnp.bfloat16), inverse[:, positions:], preferred_element_type=jnp.float32)
    mixed = (gates[2 * width :] * conv).astype(mixed_ref.dtype)
    for y in range(copies):
        mixed_ref[y] = mixed


def first_mix_kernel(live_ref, packed_ref, gain_ref, value_ref, in_ref, out_ref, *rest):
    table_ref, filt_ref, known_ref, mixed_ref, spec_ref, emit_ref = rest
    groups = packed_ref.shape[0]
    rows = value_ref.shape[1] // groups
    width = value_ref.shape[0]
    gates = square = 0.0
    for x in range(groups):
        u = packed_ref[x, :rows]
        at = pl.ds(x * rows, rows)
        w = jnp.concatenate([scaled(m, gain_ref, at) for m in (value_ref, in_ref, out_ref)], axis=0)
        gates += jnp.dot(w, u, preferred_element_type=jnp.float32)
        wide = u.astype(jnp.float32)
        square += jnp.sum(wide * wide, axis=0, keepdims=True)
        for piece in range(emit_ref.shape[1]):
            emit_ref[x, piece] = packed_ref[x, rows + piece * width : rows + (piece + 1) * width]
    square = square * (1.0 / (groups * rows))
    mix_of(gates, square, live_ref[0], table_ref, filt_ref, (), known_ref[0], mixed_ref, (spec_ref,))


def mix_kernel(tick, past, stored, features, live_ref, terms_ref, table_ref, filt_ref, *rest):
    count = past + (stored is not None)
    lagged, mixed_ref, spec_ref = rest[:count], rest[count], rest[count + 1 :]
    width = mixed_ref.shape[1]
    terms = jnp.sum(terms_ref[...].astype(jnp.float32), axis=0)
    square = (terms[3 * width : 3 * width + 1] + terms[3 * width + 1 : 3 * width + 2]) * (1.0 / features)
    known = None if stored is None else lagged[-1][stored]
    mix_of(
        terms[: 3 * width], square, live_ref[tick], table_ref, filt_ref, lagged[:past], known, mixed_ref, spec_ref
    )


def emit_terms_kernel(w_ref, mixed_ref, out_ref):
    groups, pieces, _, size = w_ref.shape
    for x in range(groups):
        term = 0.0
        for piece in range(pieces):
            rows = mixed_ref[piece * size : (piece + 1) * size]
            term += jnp.dot(w_ref[x, piece], rows, preferred_element_type=jnp.float32)
        out_ref[x] = term.astype(out_ref.dtype)


def total_of(terms_ref, own_ref):
    total = own_ref[...].astype(jnp.float32) + jnp.sum(terms_ref[...].astype(jnp.float32), axis=0)
    return total.astype(own_ref.dtype)


def spread_kernel(own_ref, *rest):
    for y in range(rest[-1].shape[0]):
        rest[-1][y] = own_ref[...]


def add_and_send_kernel(tick, layers, section_ref, terms_ref, own_ref, fresh_ref, out_ref, send_ref):
    out = total_of(terms_ref, own_ref)
    out_ref[...] = out
    send_ref[...] = jnp.where(section_ref[0] == layers - 1, fresh_ref[tick], out)


def finish_kernel(terms_ref, own_ref, *refs):
    earlier, out_ref = refs[:-1], refs[-1]
    for tick, ref in enumerate(earlier):
        out_ref[tick] = ref[...]
    out_ref[len(earlier)] = total_of(terms_ref, own_ref)


def local(feeds, newcomers, occupied, gain, value_w, in_w, out_w, emit_w, skip, filters, archive):
    section = lax.axis_index(SECTION)
    layers = lax.axis_size(SECTION)
    groups, copies = lax.axis_size("x"), lax.axis_size("y")
    ticks = newcomers.shape[0] + 1
    blocks = archive.shape[1]
    positions, width = feeds.shape[1:]
    features = gain.shape[1]
    rows = features // groups
    bf16 = functools.partial(jax.ShapeDtypeStruct, dtype=jnp.bfloat16)
    f32 = functools.partial(jax.ShapeDtypeStruct, dtype=jnp.float32)
    x = lax.axis_index("x").astype(jnp.int32)[None]
    place = section.astype(jnp.int32)[None]

    own = feeds[0].T
    part = gather_rows(jnp.broadcast_to(own[None], (copies,) + own.shape))
    gate_w = [w[0].T for w in (value_w, in_w, out_w)]
    half = filters.shape[-1] // 2
    fresh = newcomers.transpose(0, 2, 1)
    passed = [jnp.asarray(tables(positions, 2 * half)), fresh, own]
    live, known, filters, table, fresh, own = call(
        history_kernel,
        [f32((ticks, 1, positions)), bf16((blocks, 2, width, half)), f32((blocks + 1, 2, width, half))]
        + [jax.ShapeDtypeStruct(t.shape, t.dtype) for t in passed],
        [place, occupied, skip, filters[0], archive[0]] + passed,
        "history",
        smem=2,
    )

    size = rows + width * rows // positions
    packed = swap(call(pack_kernel, bf16((groups, size, positions)), [part, emit_w[0].T, live], "pack"), "x")
    mixed, spectrum, emit_rows = call(
        first_mix_kernel,
        [bf16((copies, width, positions)), f32((2, width, half)), bf16((groups, rows // positions, width, positions))],
        [live, packed, gain] + gate_w + [table, filters, known],
        "first_mix",
    )
    spectra = [spectrum]
    dealt = call(
        deal_kernel, [bf16((3 * width, rows))] * groups, [x, gain] + gate_w + [spectrum], "deal", smem=1
    )
    weights = [dealt[0]] + [
        lax.ppermute(dealt[step], "x", [(i, (i + step) % groups) for i in range(groups)]) for step in range(1, groups)
    ]

    ring = [(i, (i + 1) % layers) for i in range(layers)]
    outputs = []
    for tick in range(ticks):
        if tick > 0:
            terms = call(
                gate_terms_kernel,
                bf16((groups, 3 * width + EXTRA, positions)),
                [x, part] + weights,
                "gate_terms",
                smem=1,
            )
            terms = swap(terms, "x")
            past = min(tick, blocks)
            stored = tick if tick < blocks else None
            lagged = spectra[::-1][:past] + ([known] if stored is not None else [])
            mixed, *spectrum = call(
                functools.partial(mix_kernel, tick, past, stored, features),
                [bf16((copies, width, positions))] + [f32((2, width, half))] * (tick < ticks - 1),
                [live, terms, table, filters] + lagged,
                "mix",
            )
            spectra += spectrum
        terms = call(
            emit_terms_kernel, bf16((groups, width, positions)), [emit_rows, gather_rows(mixed)], "emit_terms"
        )
        terms = swap(terms, "x")
        if tick < ticks - 1:
            out, send = call(
                functools.partial(add_and_send_kernel, tick, layers),
                [bf16(own.shape)] * 2,
                [place, terms, own, fresh],
                "add",
                smem=1,
            )
            outputs.append(out)
            own = lax.ppermute(send, SECTION, ring)
            after = weights if tick == 0 else []
            spread = call(spread_kernel, bf16((copies,) + own.shape), [own] + after, "spread", after=len(after))
            part = gather_rows(spread)
    layer_out = call(finish_kernel, bf16((ticks,) + own.shape), [terms, own] + outputs, "finish")
    return layer_out.transpose(0, 2, 1)[None]


def solution(mesh):
    grid = Mesh(mesh.devices.reshape(8, 2, 4, 8), ("z", "core", "x", "y"))
    chan = ("x", "y")
    return jax.shard_map(
        local,
        mesh=grid,
        in_specs=(
            P(SECTION, None, chan),
            P(None, None, chan),
            P(),
            P(SECTION, None),
            P(SECTION, None, chan),
            P(SECTION, None, chan),
            P(SECTION, None, chan),
            P(SECTION, None, chan),
            P(SECTION, chan),
            P(SECTION, None, None, chan, None),
            P(SECTION, None, None, chan, None),
        ),
        out_specs=P(SECTION, None, None, chan),
        check_vma=False,
    )
```
